128 devices in a mesh: eg: 32 (over x, y, core), tp: 4 (over z).
Axes of the slice: x: 4, y: 4, z: 4, core: 2. Of those that a mesh axis runs over, the one named last changes fastest.
Arguments:
- tokens: bfloat16 [8192, 2880], P(('eg', 'tp')), may hold values from -6 to 6
- routes: int32 [8192, 4], P(('eg', 'tp')), may hold values from 0 to 127, as said below
- combine: float32 [8192, 4], P(('eg', 'tp')), may hold values from 0.1 to 0.6
- gate_values: bfloat16 [128, 1440, 2880], P('tp', 'eg'), may hold values from -0.109375 to 0.109375
- gate_scales: bfloat16 [128, 1440, 90], P('tp', 'eg'), may hold values from 0.25 to 4
- up_values: bfloat16 [128, 1440, 2880], P('tp', 'eg'), may hold values from -0.109375 to 0.109375
- up_scales: bfloat16 [128, 1440, 90], P('tp', 'eg'), may hold values from 0.25 to 4
- down_values: bfloat16 [128, 1440, 2880], P('tp', 'eg'), may hold values from -0.15625 to 0.15625
- down_scales: bfloat16 [128, 1440, 90], P('tp', 'eg'), may hold values from 0.25 to 4
Outputs:
- combined: bfloat16 [8192, 2880], P(('eg', 'tp'))
The draws below stay inside these ranges and needn't reach their ends.
Inputs may be any that keep to these rules, and one draw needn't show every extreme that they name: `routes`: each row names 4 different experts. In each aligned block of 64 rows exactly half of the experts are named, each by exactly 4 rows; one expert is named by 4 rows of every block.
All inputs are finite; a program needn't handle non-finite values.
Results may differ from the reference program's by a relative error of at most 0.0076.
Values may be sent and summed in bfloat16 or wider, within the bound.
A program may use at most 320 MiB of HBM per device.

```python
import math
import jax
import jax.numpy as jnp
from jax import lax

D = 2880
FF = 1440
TOP = 4
SCALE_BLOCK = 32
TOK_DEV = 64
EXPERTS = 128
CAP = 4
TOKENS = 8192
N_EG = 32
N_TP = 4


def draw_routes(key, part):
    key = jax.random.fold_in(key, 11)
    half_count = EXPERTS // 2
    blocks = TOKENS // TOK_DEV
    hot_key, perm_key = jax.random.split(key)
    hot_expert = jax.random.randint(hot_key, (), 0, EXPERTS).astype(jnp.int32)

    def one_block(block_key):
        order_key, shuffle_key = jax.random.split(block_key)
        others = jax.random.permutation(order_key, EXPERTS - 1).astype(jnp.int32)
        others = others + (others >= hot_expert).astype(jnp.int32)
        ordering = jnp.concatenate([hot_expert[None], others]).astype(jnp.int32)
        pair_index = jnp.arange(TOK_DEV * TOP, dtype=jnp.int32) % half_count
        chosen = ordering[pair_index].reshape(TOK_DEV, TOP)
        shuffle = jax.random.permutation(shuffle_key, TOK_DEV)
        return chosen[shuffle]
    block_keys = jax.random.split(perm_key, blocks)
    return jax.vmap(one_block)(block_keys).reshape(TOKENS, TOP).astype(jnp.int32)


def levels(own_key, dims, cuts, least, top_value):
    level, own = 1.0, jax.random.fold_in(own_key, 6)
    for position, shards_of in cuts:
        steps = jnp.exp(jax.random.uniform(jax.random.fold_in(own, position), (shards_of,), jnp.float32, least / len(cuts), top_value / len(cuts)))
        level = level * jnp.repeat(steps, dims[position] // shards_of).reshape([-1 if axis == position else 1 for axis in range(len(dims))])
    return level


def noise(stream_key, extent, deviation, limit, cuts=(), held_as=jnp.bfloat16):
    entries = jax.random.normal(stream_key, extent, jnp.float32) * deviation
    if len(cuts) > 0:
        entries = levels(stream_key, extent, cuts, -0.22, 0.18) * entries
    return jnp.clip(entries, min=-limit, max=limit).astype(held_as)


def setup_inputs(seed: int = 0) -> dict:
    splits = jax.random.split(jax.random.key(seed), 10)
    return {
        "tokens": noise(splits[0], (TOKENS, D), 1.0, 6.0, ((0, 128),)),
        "routes": draw_routes(jax.random.fold_in(splits[9], 71), 0),
        "combine": jnp.clip(0.1 + 0.5 * jax.random.uniform(splits[2], (TOKENS, TOP), jnp.float32) ** levels(splits[2], (TOKENS, TOP), ((0, 128),), -0.2, 0.2), 0.1, 0.6),
        "gate_values": noise(splits[3], (EXPERTS, FF, D), D ** -0.5, 0.109375, ((0, 4), (1, 32))),
        "gate_scales": jnp.clip(jnp.exp(math.log(4.0) - 2.7725887 * jax.random.uniform(splits[4], (EXPERTS, FF, D // SCALE_BLOCK), jnp.float32) ** levels(splits[4], (EXPERTS, FF, D // SCALE_BLOCK), ((0, 4), (1, 32)), -0.2, 0.2)), 0.25, 4.0).astype(jnp.bfloat16),
        "up_values": noise(splits[5], (EXPERTS, FF, D), D ** -0.5, 0.109375, ((0, 4), (1, 32))),
        "up_scales": jnp.clip(jnp.exp(math.log(4.0) - 2.7725887 * jax.random.uniform(splits[6], (EXPERTS, FF, D // SCALE_BLOCK), jnp.float32) ** levels(splits[6], (EXPERTS, FF, D // SCALE_BLOCK), ((0, 4), (1, 32)), -0.2, 0.2)), 0.25, 4.0).astype(jnp.bfloat16),
        "down_values": noise(splits[7], (EXPERTS, FF, D), FF ** -0.5, 0.15625, ((0, 4), (1, 32))),
        "down_scales": jnp.clip(jnp.exp(math.log(4.0) - 2.7725887 * jax.random.uniform(splits[8], (EXPERTS, FF, D // SCALE_BLOCK), jnp.float32) ** levels(splits[8], (EXPERTS, FF, D // SCALE_BLOCK), ((0, 4), (1, 32)), -0.2, 0.2)), 0.25, 4.0).astype(jnp.bfloat16),
    }


def dequantize(values, scales):
    blocks = scales.shape[-1]
    shaped = values.reshape(values.shape[:-1] + (blocks, values.shape[-1] // blocks))
    scaled = shaped.astype(jnp.float32) * scales.astype(jnp.float32)[..., None]
    return scaled.reshape(values.shape).astype(jnp.bfloat16)


def expert_ffn(picked, w_gate, w_up, w_down):
    gate_part = lax.dot_general(picked, w_gate, (((1,), (1,)), ((), ())), preferred_element_type=jnp.float32)
    upward = lax.dot_general(picked, w_up, (((1,), (1,)), ((), ())), preferred_element_type=jnp.float32)
    hidden = (jax.nn.silu(gate_part) * upward).astype(jnp.bfloat16)
    result = jnp.dot(hidden, w_down, preferred_element_type=jnp.float32)
    return result.astype(jnp.bfloat16)


def reference(tokens, routes, combine, gate_values, gate_scales, up_values, up_scales, down_values, down_scales):
    devices_all = N_EG * N_TP
    pair_count = TOK_DEV * TOP
    grouped = routes.reshape(devices_all, pair_count)
    owner_lanes = jnp.arange(EXPERTS, dtype=jnp.int32)
    hit_marks = (grouped[:, :, None] == owner_lanes[None, None, :]).astype(jnp.int32)
    earlier = jnp.cumsum(hit_marks, axis=1) - hit_marks
    pair_ranks = jnp.sum(earlier * hit_marks, axis=2).astype(jnp.int32)
    owners = jnp.broadcast_to(jnp.arange(devices_all, dtype=jnp.int32)[:, None], (devices_all, pair_count))
    token_ids = jnp.repeat(jnp.arange(TOKENS, dtype=jnp.int32).reshape(devices_all, TOK_DEV), TOP, axis=1)
    slot_table = jnp.zeros((EXPERTS, devices_all, CAP), jnp.int32).at[grouped, owners, pair_ranks].set(token_ids + 1)
    weight_table = jnp.zeros((EXPERTS, devices_all, CAP), jnp.float32).at[grouped, owners, pair_ranks].set(
        combine.reshape(devices_all, pair_count).astype(jnp.float32))

    def expert_step(running, expert):
        slot_ids = slot_table[expert].reshape(-1)
        filled = slot_ids > 0
        safe_ids = jnp.maximum(slot_ids - 1, 0).astype(jnp.int32)
        picked = jnp.where(filled[:, None], tokens[safe_ids], jnp.zeros((), tokens.dtype))
        w_gate = dequantize(gate_values[expert], gate_scales[expert])
        w_up = dequantize(up_values[expert], up_scales[expert])
        w_down = dequantize(down_values[expert], down_scales[expert])
        result = expert_ffn(picked, w_gate, w_up, w_down)
        weights = weight_table[expert].reshape(-1)
        running = running.at[safe_ids].add(weights[:, None] * result.astype(jnp.float32))
        return running, None

    finished, unused = lax.scan(expert_step, jnp.zeros((TOKENS, D), jnp.float32), jnp.arange(EXPERTS, dtype=jnp.int32))
    return finished.astype(jnp.bfloat16)
```

```python
import functools

import jax
import jax.numpy as jnp
from jax import lax
from jax.experimental import pallas as pl
from jax.experimental.pallas import tpu as pltpu
from jax.sharding import PartitionSpec as P

MESH = pl.DeviceIdType.MESH
ANY = pl.BlockSpec(memory_space=pl.ANY)
BF16, F32 = jnp.bfloat16, jnp.float32

D, FS, EXP, ROWS = 2880, 45, 32, 64
PARTS, PW = 3, 1024
FP = 48
META = 896
BLOCK = 32
VMEM = 62 * 1024 * 1024


def position():
    eg, z = lax.axis_index("eg"), lax.axis_index("tp")
    return (eg // 8, (eg // 2) % 4, z), eg % 2


def device(at, core):
    return ((at[0] * 4 + at[1]) * 2 + core, at[2])


def moved(at, axis, by):
    at = list(at)
    at[axis] = (at[axis] + by + 4) % 4
    return tuple(at)


def greet(at, core, sibling):
    barrier = pltpu.get_barrier_semaphore()
    for axis in range(3):
        for way in (1, -1):
            pl.semaphore_signal(
                barrier, inc=1, device_id=device(moved(at, axis, way), core), device_id_type=MESH
            )
    if sibling:
        pl.semaphore_signal(barrier, inc=1, device_id=device(at, 1 - core), device_id_type=MESH)
    pl.semaphore_wait(barrier, 7 if sibling else 6)


def dequantize_kernel(gv, gs, uv, us, dv, ds, out, flat):
    step = pl.program_id(0)
    width = gv.shape[-1]
    blocks = gs.shape[-1]
    lane = lax.broadcasted_iota(jnp.int32, (blocks, width), 1) + step * width
    spread = (lane // BLOCK == lax.broadcasted_iota(jnp.int32, (blocks, width), 0)).astype(BF16)
    inside = lax.broadcasted_iota(jnp.int32, (EXP, width), 1) + step * width < D
    for which, (values, scales) in enumerate(((gv, gs), (uv, us), (dv, ds))):
        def unit(f, _):
            scale = jnp.dot(scales[f], spread, preferred_element_type=F32)
            full = jnp.where(inside, values[f].astype(F32) * scale, 0.0)
            for c in range(width // 128):
                flat[c, pl.ds(f * EXP, EXP), :] = full[:, c * 128 : (c + 1) * 128]
            return 0

        lax.fori_loop(0, FS, unit, 0, unroll=5)

        def expert(e, _):
            rows = jnp.concatenate(
                [flat[c, pl.ds(e, FS, stride=EXP), :] for c in range(width // 128)], axis=1
            )
            rows = jnp.concatenate([rows, jnp.zeros((FP - FS, width), F32)], axis=0)
            out[e, which] = rows.astype(BF16)
            return 0

        lax.fori_loop(0, EXP, expert, 0, unroll=4)


def dequantize(gv, gs, uv, us, dv, ds):
    width = 512
    value = pl.BlockSpec((FS, EXP, width), lambda i: (0, 0, i))
    scale = pl.BlockSpec((FS, EXP, D // BLOCK), lambda i: (0, 0, 0))
    return pl.pallas_call(
        dequantize_kernel,
        grid=(PARTS * PW // width,),
        out_shape=jax.ShapeDtypeStruct((EXP, 3, FP, PARTS * PW), BF16),
        in_specs=[value, scale] * 3,
        out_specs=pl.BlockSpec((EXP, 3, FP, width), lambda i: (0, 0, 0, i)),
        scratch_shapes=[pltpu.VMEM((width // 128, FS * EXP, 128), F32)],
        compiler_params=pltpu.CompilerParams(vmem_limit_bytes=VMEM),
    )(gv, gs, uv, us, dv, ds)


def gather_kernel(tok, own_w, every, w1, w2, ssem, rsem, lsem, wsem):
    me, core = position()
    greet(me, core, True)
    pieces = []
    for i, (source, target, first) in enumerate(((0, w1, 0), (1, w1, 128), (2, w2, 0))):
        pieces.append(
            pltpu.make_async_remote_copy(
                own_w.at[:, source],
                target.at[:, pl.ds(first + FP, FP)],
                wsem.at[0, i],
                wsem.at[1, i],
                device_id=device(me, 1 - core),
                device_id_type=MESH,
            )
        )
        pieces.append(
            pltpu.make_async_copy(own_w.at[:, source], target.at[:, pl.ds(first, FP)], wsem.at[2, i])
        )
    for piece in pieces:
        piece.start()
    own = [
        pltpu.make_async_copy(tok.at[p], every.at[p, me[0], me[1], me[2]], lsem.at[p])
        for p in range(PARTS)
    ]
    for c in own:
        c.start()

    def region(p, phase, j, source, half):
        order = [p, (p + 1) % 3, (p + 2) % 3]
        index = [slice(None)] * 3
        index[order[phase]] = source
        if phase == 0:
            index[order[1]], index[order[2]] = me[order[1]], me[order[2]]
        elif phase == 1:
            index[order[2]] = me[order[2]]
        else:
            index[order[1]] = j
        rows = slice(None) if half is None else pl.ds(half * 32, 32)
        return every.at[(p, *index, rows)]

    def describe(p, phase, jj, way, step, arriving):
        axis = (p + phase) % 3
        back = way * (step + (1 if arriving else 0))
        source = (me[axis] - back + 8) % 4
        half = None if step == 0 else (0 if way == 1 else 1)
        j = None if phase < 2 else (me[(p + 1) % 3] + (0, -1, 1, 2)[jj] + 4) % 4
        there = region(p, phase, j, source, half)
        here = tok.at[p] if phase == 0 and step == 0 else there
        slot, kind = phase + jj, (0 if way == 1 else 1) + 2 * step
        return pltpu.make_async_remote_copy(
            here,
            there,
            ssem.at[p, slot, kind],
            rsem.at[p, slot, kind],
            device_id=device(moved(me, axis, way), core),
            device_id_type=MESH,
        )

    sent = []

    def go(p, phase, jj, way, step):
        c = describe(p, phase, jj, way, step, False)
        c.start()
        sent.append(c)

    def arrive(p, phase, jj, way, step):
        describe(p, phase, jj, way, step, True).wait_recv()

    parts, ways = range(PARTS), (1, -1)
    for p in parts:
        for way in ways:
            go(p, 0, 0, way, 0)
    for p in parts:
        for way in ways:
            arrive(p, 0, 0, way, 0)
            go(p, 0, 0, way, 1)
    for c in own:
        c.wait()
    for p in parts:
        for way in ways:
            arrive(p, 0, 0, way, 1)
        for way in ways:
            go(p, 1, 0, way, 0)
    for p in parts:
        for way in ways:
            go(p, 2, 0, way, 0)
    for p in parts:
        for way in ways:
            arrive(p, 1, 0, way, 0)
            go(p, 1, 0, way, 1)
    for p in parts:
        for jj in (1, 2):
            for way in ways:
                go(p, 2, jj, way, 0)
    for p in parts:
        for way in ways:
            arrive(p, 1, 0, way, 1)
        for way in ways:
            go(p, 2, 3, way, 0)
    for jj in range(4):
        for p in parts:
            for way in ways:
                arrive(p, 2, jj, way, 0)
                go(p, 2, jj, way, 1)
    for jj in range(4):
        for p in parts:
            for way in ways:
                arrive(p, 2, jj, way, 1)
    for c in sent:
        c.wait_send()
    for piece in pieces:
        piece.wait()


def gather(tok, own_w):
    return pl.pallas_call(
        gather_kernel,
        out_shape=[
            jax.ShapeDtypeStruct((PARTS, 4, 4, 4, ROWS, PW), BF16),
            jax.ShapeDtypeStruct((EXP, 256, PARTS * PW), BF16),
            jax.ShapeDtypeStruct((EXP, 2 * FP, PARTS * PW), BF16),
        ],
        in_specs=[ANY] * 2,
        out_specs=[ANY] * 3,
        scratch_shapes=[
            pltpu.SemaphoreType.DMA((PARTS, 6, 4)),
            pltpu.SemaphoreType.DMA((PARTS, 6, 4)),
            pltpu.SemaphoreType.DMA((PARTS,)),
            pltpu.SemaphoreType.DMA((3, 3)),
        ],
        compiler_params=pltpu.CompilerParams(collective_id=1, has_side_effects=True),
    )(tok, own_w)


PER_STEP = 4


def upward_kernel(every, meta, w1, hidden, place, rows, acc):
    p, step = pl.program_id(0), pl.program_id(1)
    z = lax.axis_index("tp")

    @pl.when((p == 0) & (step == 0))
    def _():
        slots = lax.broadcasted_iota(jnp.int32, (ROWS, EXP * 16), 1).astype(F32)

        def block(i, _):
            g, b = i // 4, i % 4
            m = meta[0, g // 4, g % 4, b].astype(F32)
            local = m[:, 0:4] - (z * EXP).astype(F32)
            ids = local * 16.0 + b.astype(F32) * 4.0 + m[:, 4:8]
            ids = jnp.where((local >= 0.0) & (local < EXP), ids, -1.0)
            hit = slots == ids[:, 0:1]
            for k in range(1, 4):
                hit = hit | (slots == ids[:, k : k + 1])
            place[g, pl.ds(b * ROWS, ROWS), :] = hit.astype(F32).astype(BF16)
            return 0

        lax.fori_loop(0, 64, block, 0)

    @pl.when(step == 0)
    def _():
        def group(g, _):
            x = every[0, g // 4, g % 4].reshape(4 * ROWS, PW)
            picked = lax.dot_general(
                place[g], x, (((0,), (0,)), ((), ())), preferred_element_type=F32
            )
            rows[:, pl.ds(g * 16, 16), :] = picked.astype(BF16).reshape(EXP, 16, PW)
            return 0

        lax.fori_loop(0, 16, group, 0)

    for i in range(PER_STEP):
        e = step * PER_STEP + i
        out = lax.dot_general(
            rows[e], w1[i], (((1,), (1,)), ((), ())), preferred_element_type=F32
        )

        @pl.when(p == 0)
        def _():
            acc[e] = out

        @pl.when(p == 1)
        def _():
            acc[e] += out

        @pl.when(p == 2)
        def _():
            total = acc[e] + out
            gate, up = total[:, :128], total[:, 128:]
            made = gate / (1.0 + jnp.exp(-gate)) * up
            m = rows[e, :, META:].astype(F32)
            named = (m[:, 0:4] == (z * EXP + e).astype(F32)).astype(F32)
            weights = [
                jnp.sum(m[:, 8 + 4 * i : 12 + 4 * i] * named, axis=1, keepdims=True)
                for i in range(3)
            ]
            lane = lax.broadcasted_iota(jnp.int32, made.shape, 1)
            for i in range(3):
                made = jnp.where(lane == 96 + i, weights[i], made)
            made = jnp.where(lane > 98, 0.0, made)
            hidden[e] = made.astype(BF16)


def upward(every, w1):
    return pl.pallas_call(
        upward_kernel,
        grid=(PARTS, EXP // PER_STEP),
        out_shape=[
            jax.ShapeDtypeStruct((EXP, 256, 128), BF16),
            jax.ShapeDtypeStruct((16, 4 * ROWS, EXP * 16), BF16),
        ],
        in_specs=[
            pl.BlockSpec((1, 4, 4, 4, ROWS, PW), lambda p, s: (p, 0, 0, 0, 0, 0)),
            pl.BlockSpec((1, 4, 4, 4, ROWS, 128), lambda p, s: (2, 0, 0, 0, 0, 7)),
            pl.BlockSpec((PER_STEP, 256, PW), lambda p, s: (s, 0, p)),
        ],
        out_specs=[
            pl.BlockSpec((EXP, 256, 128), lambda p, s: (0, 0, 0)),
            pl.BlockSpec((16, 4 * ROWS, EXP * 16), lambda p, s: (0, 0, 0)),
        ],
        scratch_shapes=[
            pltpu.VMEM((EXP, 256, PW), BF16),
            pltpu.VMEM((EXP, 256, 256), F32),
        ],
        compiler_params=pltpu.CompilerParams(vmem_limit_bytes=VMEM),
    )(every, every, w1)


def downward_kernel(hidden, place, w2, out, results):
    step = pl.program_id(1)
    for i in range(PER_STEP):
        e = step * PER_STEP + i
        h = hidden[e]
        w = h[:, 96:99].astype(F32)
        w = (w[:, 0:1] + w[:, 1:2]) + w[:, 2:3]
        y = jnp.dot(h[:, : 2 * FP], w2[i], preferred_element_type=F32) * w
        results[:, pl.ds(e * 16, 16), :] = y.astype(BF16).reshape(16, 16, PW)

    @pl.when(step == EXP // PER_STEP - 1)
    def _():
        def group(g, _):
            summed = jnp.dot(place[g], results[g], preferred_element_type=F32)
            out[0, g // 4, g % 4] = summed.astype(BF16).reshape(4, ROWS, PW)
            return 0

        lax.fori_loop(0, 16, group, 0)


def downward(hidden, place, w2):
    return pl.pallas_call(
        downward_kernel,
        grid=(PARTS, EXP // PER_STEP),
        out_shape=jax.ShapeDtypeStruct((PARTS, 4, 4, 4, ROWS, PW), BF16),
        in_specs=[
            pl.BlockSpec((EXP, 256, 128), lambda p, s: (0, 0, 0)),
            pl.BlockSpec((16, 4 * ROWS, EXP * 16), lambda p, s: (0, 0, 0)),
            pl.BlockSpec((PER_STEP, 2 * FP, PW), lambda p, s: (s, 0, p)),
        ],
        out_specs=pl.BlockSpec((1, 4, 4, 4, ROWS, PW), lambda p, s: (p, 0, 0, 0, 0, 0)),
        scratch_shapes=[pltpu.VMEM((16, EXP * 16, PW), BF16)],
        compiler_params=pltpu.CompilerParams(vmem_limit_bytes=VMEM),
    )(hidden, place, w2)


def scatter_kernel(part, out, far0, near0, mid0, acc, far1, near1, far2, near2, own2, sems, lsem):
    me, core = position()
    greet(me, core, False)
    parts = range(PARTS)
    sent = []

    def copy(here, there, p, phase, jj, kind, way, axis):
        return pltpu.make_async_remote_copy(
            here,
            there,
            sems.at[0, p, phase + jj, kind],
            sems.at[1, p, phase + jj, kind],
            device_id=device(moved(me, axis, way), core),
            device_id_type=MESH,
        )

    def go(*a):
        c = copy(*a)
        c.start()
        sent.append(c)

    def j_of(p, jj):
        return (me[(p + 1) % 3] + (2, 1, -1, 0)[jj] + 4) % 4

    def piece(p, jj, by, rows):
        o0, o1, o2 = p, (p + 1) % 3, (p + 2) % 3
        index = [slice(None)] * 3
        index[o1] = j_of(p, jj)
        index[o2] = (me[o2] + by + 4) % 4
        return part.at[(p, *index, rows)]

    top, bottom, whole = pl.ds(0, 32), pl.ds(32, 32), slice(None)

    def load(p, jj, k):
        by, rows = ((1, top), (-1, bottom), (0, whole))[k]
        there = acc.at[p, jj] if k == 2 else mid0.at[p, jj, k]
        return pltpu.make_async_copy(piece(p, jj, by, rows), there, lsem.at[p, jj, k])

    def issue(jj):
        for p in parts:
            axis = (p + 2) % 3
            go(piece(p, jj, 2, top), far0.at[p, jj, 0], p, 0, jj, 0, 1, axis)
            go(piece(p, jj, 2, bottom), far0.at[p, jj, 1], p, 0, jj, 1, -1, axis)
            for k in range(3):
                load(p, jj, k).start()
        for p in parts:
            axis = (p + 2) % 3
            go(piece(p, jj, 1, bottom), near0.at[p, jj, 0, :, bottom], p, 0, jj, 2, 1, axis)
            go(piece(p, jj, -1, top), near0.at[p, jj, 1, :, top], p, 0, jj, 3, -1, axis)

    def wait_in(there, p, phase, jj, kind, axis):
        copy(there, there, p, phase, jj, kind, 1, axis).wait_recv()

    def add(target, *others):
        count = target.shape[0]

        def one(i, _):
            total = target[i].astype(F32)
            for other in others:
                total = total + other[i].astype(F32)
            target[i] = total.astype(BF16)
            return 0

        lax.fori_loop(0, count, one, 0)

    def middle(jj):
        for p in parts:
            axis = (p + 2) % 3
            for k, way in ((0, 1), (1, -1)):
                half = top if k == 0 else bottom
                load(p, jj, k).wait()
                wait_in(far0.at[p, jj, k], p, 0, jj, k, axis)
                add(mid0.at[p, jj, k], far0.at[p, jj, k])
                go(mid0.at[p, jj, k], near0.at[p, jj, k, :, half], p, 0, jj, 4 + k, way, axis)

    def finish(jj):
        for p in parts:
            axis = (p + 2) % 3
            load(p, jj, 2).wait()
            wait_in(near0.at[p, jj, 0, :, bottom], p, 0, jj, 2, axis)
            wait_in(near0.at[p, jj, 1, :, top], p, 0, jj, 3, axis)
            wait_in(near0.at[p, jj, 0, :, top], p, 0, jj, 4, axis)
            wait_in(near0.at[p, jj, 1, :, bottom], p, 0, jj, 5, axis)
            add(acc.at[p, jj], near0.at[p, jj, 0], near0.at[p, jj, 1])
            axis = (p + 1) % 3
            if jj == 0:
                go(acc.at[p, 0, :, top], far1.at[p, 0], p, 4, 0, 0, 1, axis)
                go(acc.at[p, 0, :, bottom], far1.at[p, 1], p, 4, 0, 1, -1, axis)
            elif jj == 1:
                go(acc.at[p, 1, :, bottom], near1.at[p, 0, :, bottom], p, 4, 0, 2, 1, axis)
            elif jj == 2:
                go(acc.at[p, 2, :, top], near1.at[p, 1, :, top], p, 4, 0, 3, -1, axis)
        if jj in (1, 2):
            k, way, half = (0, 1, top) if jj == 1 else (1, -1, bottom)
            for p in parts:
                axis = (p + 1) % 3
                wait_in(far1.at[p, k], p, 4, 0, k, axis)
                add(acc.at[p, jj, :, half], far1.at[p, k])
                go(acc.at[p, jj, :, half], near1.at[p, k, :, half], p, 4, 0, 4 + k, way, axis)

    issue(0)
    issue(1)
    for jj in range(4):
        middle(jj)
        if jj + 2 < 4:
            issue(jj + 2)
        if jj >= 1:
            finish(jj - 1)
    finish(3)
    for p in parts:
        axis = (p + 1) % 3
        wait_in(near1.at[p, 0, :, bottom], p, 4, 0, 2, axis)
        wait_in(near1.at[p, 1, :, top], p, 4, 0, 3, axis)
        wait_in(near1.at[p, 0, :, top], p, 4, 0, 4, axis)
        wait_in(near1.at[p, 1, :, bottom], p, 4, 0, 5, axis)
        add(acc.at[p, 3], near1.at[p, 0], near1.at[p, 1])
        t = [(me[p] + by + 4) % 4 for by in (2, 1, -1, 0)]
        go(acc.at[p, 3, t[0], top], far2.at[p, 0], p, 5, 0, 0, 1, p)
        go(acc.at[p, 3, t[0], bottom], far2.at[p, 1], p, 5, 0, 1, -1, p)
        go(acc.at[p, 3, t[1], bottom], near2.at[p, 0, bottom], p, 5, 0, 2, 1, p)
        go(acc.at[p, 3, t[2], top], near2.at[p, 1, top], p, 5, 0, 3, -1, p)
    for p in parts:
        t = [(me[p] + by + 4) % 4 for by in (2, 1, -1, 0)]
        for k, way, half in ((0, 1, top), (1, -1, bottom)):
            wait_in(far2.at[p, k], p, 5, 0, k, p)
            own2[p, k] = (
                acc[p, 3, t[1 + k], half].astype(F32) + far2[p, k].astype(F32)
            ).astype(BF16)
            go(own2.at[p, k], near2.at[p, k, half], p, 5, 0, 4 + k, way, p)
    for p in parts:
        wait_in(near2.at[p, 0, bottom], p, 5, 0, 2, p)
        wait_in(near2.at[p, 1, top], p, 5, 0, 3, p)
        wait_in(near2.at[p, 0, top], p, 5, 0, 4, p)
        wait_in(near2.at[p, 1, bottom], p, 5, 0, 5, p)
        out[p] = (
            acc[p, 3, me[p]].astype(F32) + near2[p, 0].astype(F32) + near2[p, 1].astype(F32)
        ).astype(BF16)
    for c in sent:
        c.wait_send()


def scatter(part):
    half = ROWS // 2
    return pl.pallas_call(
        scatter_kernel,
        out_shape=jax.ShapeDtypeStruct((PARTS, ROWS, PW), BF16),
        in_specs=[ANY],
        out_specs=pl.BlockSpec(memory_space=pltpu.VMEM),
        scratch_shapes=[
            pltpu.VMEM((PARTS, 4, 2, 4, half, PW), BF16),
            pltpu.VMEM((PARTS, 4, 2, 4, ROWS, PW), BF16),
            pltpu.VMEM((PARTS, 4, 2, 4, half, PW), BF16),
            pltpu.VMEM((PARTS, 4, 4, ROWS, PW), BF16),
            pltpu.VMEM((PARTS, 2, 4, half, PW), BF16),
            pltpu.VMEM((PARTS, 2, 4, ROWS, PW), BF16),
            pltpu.VMEM((PARTS, 2, half, PW), BF16),
            pltpu.VMEM((PARTS, 2, ROWS, PW), BF16),
            pltpu.VMEM((PARTS, 2, half, PW), BF16),
            pltpu.SemaphoreType.DMA((2, PARTS, 6, 6)),
            pltpu.SemaphoreType.DMA((PARTS, 4, 3)),
        ],
        compiler_params=pltpu.CompilerParams(
            collective_id=2, has_side_effects=True, vmem_limit_bytes=VMEM
        ),
    )(part)


def with_meta(tokens, routes, combine):
    flat = routes.reshape(-1)
    index = jnp.arange(flat.shape[0], dtype=jnp.int32)
    same = (flat[:, None] == flat[None, :]) & (index[None, :] < index[:, None])
    rank = jnp.sum(same.astype(jnp.int32), axis=1).reshape(routes.shape)
    high = lax.reduce_precision(combine, 8, 7)
    rest = combine - high
    middle = lax.reduce_precision(rest, 8, 7)
    low = rest - middle
    columns = [routes.astype(F32), rank.astype(F32), high, middle, low]
    meta = jnp.concatenate(columns + [jnp.zeros((ROWS, 128 - 20), F32)], axis=1).astype(BF16)
    pad = jnp.zeros((ROWS, PARTS * PW - 128 - D), BF16)
    wide = jnp.concatenate([tokens, pad, meta], axis=1)
    return wide.reshape(ROWS, PARTS, PW).transpose(1, 0, 2)


def local(tokens, routes, combine, gv, gs, uv, us, dv, ds):
    weights = [w.transpose(1, 0, 2) for w in (gv, gs, uv, us, dv, ds)]
    own_w = dequantize(*weights)
    every, w1, w2 = gather(with_meta(tokens, routes, combine), own_w)
    hidden, place = upward(every, w1)
    partial = downward(hidden, place, w2)
    result = scatter(partial)
    return result.transpose(1, 0, 2).reshape(ROWS, PARTS * PW)[:, :D]


def solution(mesh):
    rows = P(("eg", "tp"), None)
    weight = P("tp", "eg", None)
    return jax.shard_map(
        local,
        mesh=mesh,
        in_specs=(rows, rows, rows) + (weight,) * 6,
        out_specs=rows,
        check_vma=False,
    )
```

```python
import functools

import jax
import jax.numpy as jnp
from jax import lax
from jax.experimental import pallas as pl
from jax.experimental.pallas import tpu as pltpu
from jax.sharding import PartitionSpec as P

MESH = pl.DeviceIdType.MESH
ANY = pl.BlockSpec(memory_space=pl.ANY)
BF16, F32 = jnp.bfloat16, jnp.float32

D, FS, EXP, ROWS = 2880, 45, 32, 64
PARTS, PW = 3, 1024
FP = 48
META = 896
BLOCK = 32
VMEM = 62 * 1024 * 1024


def position():
    eg, z = lax.axis_index("eg"), lax.axis_index("tp")
    return (eg // 8, (eg // 2) % 4, z), eg % 2


def device(at, core):
    return ((at[0] * 4 + at[1]) * 2 + core, at[2])


def moved(at, axis, by):
    at = list(at)
    at[axis] = (at[axis] + by + 4) % 4
    return tuple(at)


def greet(at, core, sibling):
    barrier = pltpu.get_barrier_semaphore()
    for axis in range(3):
        for way in (1, -1):
            pl.semaphore_signal(
                barrier, inc=1, device_id=device(moved(at, axis, way), core), device_id_type=MESH
            )
    if sibling:
        pl.semaphore_signal(barrier, inc=1, device_id=device(at, 1 - core), device_id_type=MESH)
    pl.semaphore_wait(barrier, 7 if sibling else 6)


WIDE = 512
PIECES = 3 * PARTS * PW // WIDE
PITCH = EXP + 1


def gather_kernel(
    tok, gv, gs, uv, us, dv, ds, every, weights, raw, scales, flat, made, ssem, rsem, lsem, wsem, dsem
):
    me, core = position()
    fetched = []
    for i, (values, scale) in enumerate(((gv, gs), (uv, us), (dv, ds))):
        fetched.append(pltpu.make_async_copy(values, raw.at[i], dsem.at[2 * i]))
        fetched.append(pltpu.make_async_copy(scale, scales.at[i], dsem.at[2 * i + 1]))
    for c in fetched:
        c.start()
    greet(me, core, True)

    def target(n, first):
        start = pl.multiple_of(n // 3 * WIDE, WIDE)
        return weights.at[:, n % 3, pl.ds(first, FP), pl.ds(start, WIDE)]

    def keep(n):
        return pltpu.make_async_copy(made.at[n % 2], target(n, 0), wsem.at[2, n % 2])

    def give(n):
        return pltpu.make_async_remote_copy(
            made.at[n % 2],
            target(n, FP),
            wsem.at[0, n % 2],
            wsem.at[1, n],
            device_id=device(me, 1 - core),
            device_id_type=MESH,
        )

    def dequantize(column, which):
        n = column * 3 + which
        slot = n % 2

        @pl.when(n >= 2)
        def _():
            keep(n - 2).wait()
            give(n - 2).wait_send()

        start = column * WIDE
        real = min(WIDE, D - start)
        blocks = D // BLOCK
        lane = lax.broadcasted_iota(jnp.int32, (blocks, WIDE), 1) + start
        spread = (lane // BLOCK == lax.broadcasted_iota(jnp.int32, (blocks, WIDE), 0)).astype(BF16)
        def units(i, _):
            count = 5
            scale = jnp.dot(
                scales[which, pl.ds(i * count, count)].reshape(count * EXP, blocks),
                spread,
                preferred_element_type=F32,
            )
            values = raw[which, pl.ds(i * count, count), :, pl.ds(start, real)]
            full = values.reshape(count * EXP, real).astype(F32) * scale[:, :real]
            if real < WIDE:
                full = jnp.concatenate([full, jnp.zeros((count * EXP, WIDE - real), F32)], axis=1)
            for c in range(WIDE // 128):
                for k in range(count):
                    flat[c, pl.ds((i * count + k) * PITCH, EXP), :] = full[
                        k * EXP : (k + 1) * EXP, c * 128 : (c + 1) * 128
                    ]
            return 0

        lax.fori_loop(0, FS // 5, units, 0)

        def expert(e, _):
            for c in range(WIDE // 128):
                rows = flat[c, pl.ds(e, FS, stride=PITCH), :]
                rows = jnp.concatenate([rows, jnp.zeros((FP - FS, 128), F32)], axis=0)
                made[slot, e, :, pl.ds(c * 128, 128)] = rows.astype(BF16)
            return 0

        lax.fori_loop(0, EXP, expert, 0, unroll=4)
        keep(n).start()
        give(n).start()

    def work(*columns):
        for column in columns:
            lax.fori_loop(0, 3, lambda which, _: dequantize(column, which) or 0, 0)

    own = [
        pltpu.make_async_copy(tok.at[p], every.at[p, me[0], me[1], me[2]], lsem.at[p])
        for p in range(PARTS)
    ]
    for c in own:
        c.start()

    def region(p, phase, j, source, half):
        order = [p, (p + 1) % 3, (p + 2) % 3]
        index = [slice(None)] * 3
        index[order[phase]] = source
        if phase == 0:
            index[order[1]], index[order[2]] = me[order[1]], me[order[2]]
        elif phase == 1:
            index[order[2]] = me[order[2]]
        else:
            index[order[1]] = j
        rows = slice(None) if half is None else pl.ds(half * 32, 32)
        return every.at[(p, *index, rows)]

    def describe(p, phase, jj, way, step, arriving):
        axis = (p + phase) % 3
        back = way * (step + (1 if arriving else 0))
        source = (me[axis] - back + 8) % 4
        half = None if step == 0 else (0 if way == 1 else 1)
        j = None if phase < 2 else (me[(p + 1) % 3] + (0, -1, 1, 2)[jj] + 4) % 4
        there = region(p, phase, j, source, half)
        here = tok.at[p] if phase == 0 and step == 0 else there
        slot, kind = phase + jj, (0 if way == 1 else 1) + 2 * step
        return pltpu.make_async_remote_copy(
            here,
            there,
            ssem.at[p, slot, kind],
            rsem.at[p, slot, kind],
            device_id=device(moved(me, axis, way), core),
            device_id_type=MESH,
        )

    sent = []

    def go(p, phase, jj, way, step):
        c = describe(p, phase, jj, way, step, False)
        c.start()
        sent.append(c)

    def arrive(p, phase, jj, way, step):
        describe(p, phase, jj, way, step, True).wait_recv()

    parts, ways = range(PARTS), (1, -1)
    for p in parts:
        for way in ways:
            go(p, 0, 0, way, 0)
    for c in fetched:
        c.wait()
    for p in parts:
        for way in ways:
            arrive(p, 0, 0, way, 0)
            go(p, 0, 0, way, 1)
    for c in own:
        c.wait()
    for p in parts:
        for way in ways:
            arrive(p, 0, 0, way, 1)
        for way in ways:
            go(p, 1, 0, way, 0)
    for p in parts:
        for way in ways:
            go(p, 2, 0, way, 0)
    for p in parts:
        for way in ways:
            arrive(p, 1, 0, way, 0)
            go(p, 1, 0, way, 1)
    for p in parts:
        for jj in (1, 2):
            for way in ways:
                go(p, 2, jj, way, 0)
    for p in parts:
        for way in ways:
            arrive(p, 1, 0, way, 1)
        for way in ways:
            go(p, 2, 3, way, 0)
    for jj in range(4):
        work(*((0, 1), (2,), (3,), (4,))[jj])
        for p in parts:
            for way in ways:
                arrive(p, 2, jj, way, 0)
                go(p, 2, jj, way, 1)
    work(5)
    for jj in range(4):
        for p in parts:
            for way in ways:
                arrive(p, 2, jj, way, 1)
    for c in sent:
        c.wait_send()
    for n in (PIECES - 2, PIECES - 1):
        keep(n).wait()
        give(n).wait_send()

    def received(n, _):
        give(n).wait_recv()
        return 0

    lax.fori_loop(0, PIECES, received, 0)


def gather(tok, *weights):
    return pl.pallas_call(
        gather_kernel,
        out_shape=[
            jax.ShapeDtypeStruct((PARTS, 4, 4, 4, ROWS, PW), BF16),
            jax.ShapeDtypeStruct((EXP, 3, 2 * FP, PARTS * PW), BF16),
        ],
        in_specs=[ANY] * 7,
        out_specs=[ANY] * 2,
        scratch_shapes=[
            pltpu.VMEM((3, FS, EXP, D), BF16),
            pltpu.VMEM((3, FS, EXP, D // BLOCK), BF16),
            pltpu.VMEM((WIDE // 128, FS * PITCH, 128), F32),
            pltpu.VMEM((2, EXP, FP, WIDE), BF16),
            pltpu.SemaphoreType.DMA((PARTS, 6, 4)),
            pltpu.SemaphoreType.DMA((PARTS, 6, 4)),
            pltpu.SemaphoreType.DMA((PARTS,)),
            pltpu.SemaphoreType.DMA((3, PIECES)),
            pltpu.SemaphoreType.DMA((6,)),
        ],
        compiler_params=pltpu.CompilerParams(
            collective_id=1, has_side_effects=True, vmem_limit_bytes=VMEM
        ),
    )(tok, *weights)


PER_STEP = 4


def upward_kernel(every, meta, weights, hidden, place, rows, acc):
    p, step = pl.program_id(0), pl.program_id(1)
    z = lax.axis_index("tp")

    @pl.when((p == 0) & (step == 0))
    def _():
        slots = lax.broadcasted_iota(jnp.int32, (ROWS, EXP * 16), 1).astype(F32)

        def block(i, _):
            g, b = i // 4, i % 4
            m = meta[0, g // 4, g % 4, b].astype(F32)
            local = m[:, 64:68] - (z * EXP).astype(F32)
            ids = local * 16.0 + b.astype(F32) * 4.0 + m[:, 80:84]
            ids = jnp.where((local >= 0.0) & (local < EXP), ids, -1.0)
            hit = slots == ids[:, 0:1]
            for k in range(1, 4):
                hit = hit | (slots == ids[:, k : k + 1])
            place[g, pl.ds(b * ROWS, ROWS), :] = hit.astype(F32).astype(BF16)
            return 0

        lax.fori_loop(0, 64, block, 0)

        def clear(e, _):
            acc[e] = jnp.zeros((256, 256), F32)
            return 0

        lax.fori_loop(0, EXP, clear, 0)

    @pl.when(step == 0)
    def _():
        def group(g, _):
            x = every[0, g // 4, g % 4].reshape(4 * ROWS, PW)
            picked = lax.dot_general(
                place[g], x, (((0,), (0,)), ((), ())), preferred_element_type=F32
            )
            rows[:, pl.ds(g * 16, 16), :] = picked.astype(BF16).reshape(EXP, 16, PW)
            return 0

        lax.fori_loop(0, 16, group, 0)

    for i in range(PER_STEP):
        e = step * PER_STEP + i
        acc[e, :, pl.ds(0, 4 * FP)] += lax.dot_general(
            rows[e],
            weights[i].reshape(4 * FP, PW),
            (((1,), (1,)), ((), ())),
            preferred_element_type=F32,
        )

    @pl.when(p == PARTS - 1)
    def _():
        ones = jnp.ones((128, 128), BF16)
        lane = lax.broadcasted_iota(jnp.int32, (256, 128), 1)
        for i in range(PER_STEP):
            e = step * PER_STEP + i
            total = acc[e]
            gate, up = total[:, :128], pltpu.roll(total, 128 - 2 * FP, 1)[:, 128:]
            m = rows[e, :, META:].astype(F32)
            named = pltpu.roll(m, 64, 1) == (z * EXP + e).astype(F32)
            chosen = jnp.where(named & (lane < 12), m, 0.0).astype(BF16)
            weight = jnp.dot(chosen, ones, preferred_element_type=F32)
            value = gate / (1.0 + jnp.exp(-gate)) * up * weight
            hidden[e] = value.astype(BF16)


def upward(every, weights):
    return pl.pallas_call(
        upward_kernel,
        grid=(PARTS, EXP // PER_STEP),
        out_shape=[
            jax.ShapeDtypeStruct((EXP, 256, 128), BF16),
            jax.ShapeDtypeStruct((16, 4 * ROWS, EXP * 16), BF16),
        ],
        in_specs=[
            pl.BlockSpec((1, 4, 4, 4, ROWS, PW), lambda p, s: (p, 0, 0, 0, 0, 0)),
            pl.BlockSpec((1, 4, 4, 4, ROWS, 128), lambda p, s: (2, 0, 0, 0, 0, 7)),
            pl.BlockSpec((PER_STEP, 2, 2 * FP, PW), lambda p, s: (s, 0, 0, p)),
        ],
        out_specs=[
            pl.BlockSpec((EXP, 256, 128), lambda p, s: (0, 0, 0)),
            pl.BlockSpec((16, 4 * ROWS, EXP * 16), lambda p, s: (0, 0, 0)),
        ],
        scratch_shapes=[
            pltpu.VMEM((EXP, 256, PW), BF16),
            pltpu.VMEM((EXP, 256, 256), F32),
        ],
        compiler_params=pltpu.CompilerParams(vmem_limit_bytes=VMEM),
    )(every, every, weights)


def downward_kernel(hidden, place, w2, out, results):
    step = pl.program_id(1)
    for i in range(PER_STEP):
        e = step * PER_STEP + i
        y = jnp.dot(hidden[e, :, : 2 * FP], w2[i, 0], preferred_element_type=F32)
        results[:, pl.ds(e * 16, 16), :] = y.astype(BF16).reshape(16, 16, PW)

    @pl.when(step == EXP // PER_STEP - 1)
    def _():
        def group(g, _):
            summed = jnp.dot(place[g], results[g], preferred_element_type=F32)
            out[0, g // 4, g % 4] = summed.astype(BF16).reshape(4, ROWS, PW)
            return 0

        lax.fori_loop(0, 16, group, 0)


def downward(hidden, place, w2):
    return pl.pallas_call(
        downward_kernel,
        grid=(PARTS, EXP // PER_STEP),
        out_shape=jax.ShapeDtypeStruct((PARTS, 4, 4, 4, ROWS, PW), BF16),
        in_specs=[
            pl.BlockSpec((EXP, 256, 128), lambda p, s: (0, 0, 0)),
            pl.BlockSpec((16, 4 * ROWS, EXP * 16), lambda p, s: (0, 0, 0)),
            pl.BlockSpec((PER_STEP, 1, 2 * FP, PW), lambda p, s: (s, 2, 0, p)),
        ],
        out_specs=pl.BlockSpec((1, 4, 4, 4, ROWS, PW), lambda p, s: (p, 0, 0, 0, 0, 0)),
        scratch_shapes=[pltpu.VMEM((16, EXP * 16, PW), BF16)],
        compiler_params=pltpu.CompilerParams(vmem_limit_bytes=VMEM),
    )(hidden, place, w2)


def scatter_kernel(part, out, far0, near0, mid0, acc, far1, near1, far2, near2, own2, sems, lsem):
    me, core = position()
    greet(me, core, False)
    parts = range(PARTS)
    sent = []

    def copy(here, there, p, phase, jj, kind, way, axis):
        return pltpu.make_async_remote_copy(
            here,
            there,
            sems.at[0, p, phase + jj, kind],
            sems.at[1, p, phase + jj, kind],
            device_id=device(moved(me, axis, way), core),
            device_id_type=MESH,
        )

    def go(*a):
        c = copy(*a)
        c.start()
        sent.append(c)

    def j_of(p, jj):
        return (me[(p + 1) % 3] + (2, 1, -1, 0)[jj] + 4) % 4

    def piece(p, jj, by, rows):
        o0, o1, o2 = p, (p + 1) % 3, (p + 2) % 3
        index = [slice(None)] * 3
        index[o1] = j_of(p, jj)
        index[o2] = (me[o2] + by + 4) % 4
        return part.at[(p, *index, rows)]

    top, bottom, whole = pl.ds(0, 32), pl.ds(32, 32), slice(None)

    def load(p, jj, k):
        by, rows = ((1, top), (-1, bottom), (0, whole))[k]
        there = acc.at[p, jj] if k == 2 else mid0.at[p, jj, k]
        return pltpu.make_async_copy(piece(p, jj, by, rows), there, lsem.at[p, jj, k])

    def issue(jj):
        for p in parts:
            axis = (p + 2) % 3
            go(piece(p, jj, 2, top), far0.at[p, jj, 0], p, 0, jj, 0, 1, axis)
            go(piece(p, jj, 2, bottom), far0.at[p, jj, 1], p, 0, jj, 1, -1, axis)
            for k in range(3):
                load(p, jj, k).start()
        for p in parts:
            axis = (p + 2) % 3
            go(piece(p, jj, 1, bottom), near0.at[p, jj, 0, :, bottom], p, 0, jj, 2, 1, axis)
            go(piece(p, jj, -1, top), near0.at[p, jj, 1, :, top], p, 0, jj, 3, -1, axis)

    def wait_in(there, p, phase, jj, kind, axis):
        copy(there, there, p, phase, jj, kind, 1, axis).wait_recv()

    def add(target, *others):
        count = target.shape[0]

        def one(i, _):
            total = target[i].astype(F32)
            for other in others:
                total = total + other[i].astype(F32)
            target[i] = total.astype(BF16)
            return 0

        lax.fori_loop(0, count, one, 0)

    def middle(jj):
        for p in parts:
            axis = (p + 2) % 3
            for k, way in ((0, 1), (1, -1)):
                half = top if k == 0 else bottom
                load(p, jj, k).wait()
                wait_in(far0.at[p, jj, k], p, 0, jj, k, axis)
                add(mid0.at[p, jj, k], far0.at[p, jj, k])
                go(mid0.at[p, jj, k], near0.at[p, jj, k, :, half], p, 0, jj, 4 + k, way, axis)

    def finish(jj):
        for p in parts:
            axis = (p + 2) % 3
            load(p, jj, 2).wait()
            wait_in(near0.at[p, jj, 0, :, bottom], p, 0, jj, 2, axis)
            wait_in(near0.at[p, jj, 1, :, top], p, 0, jj, 3, axis)
            wait_in(near0.at[p, jj, 0, :, top], p, 0, jj, 4, axis)
            wait_in(near0.at[p, jj, 1, :, bottom], p, 0, jj, 5, axis)
            add(acc.at[p, jj], near0.at[p, jj, 0], near0.at[p, jj, 1])
            axis = (p + 1) % 3
            if jj == 0:
                go(acc.at[p, 0, :, top], far1.at[p, 0], p, 4, 0, 0, 1, axis)
                go(acc.at[p, 0, :, bottom], far1.at[p, 1], p, 4, 0, 1, -1, axis)
            elif jj == 1:
                go(acc.at[p, 1, :, bottom], near1.at[p, 0, :, bottom], p, 4, 0, 2, 1, axis)
            elif jj == 2:
                go(acc.at[p, 2, :, top], near1.at[p, 1, :, top], p, 4, 0, 3, -1, axis)
        if jj in (1, 2):
            k, way, half = (0, 1, top) if jj == 1 else (1, -1, bottom)
            for p in parts:
                axis = (p + 1) % 3
                wait_in(far1.at[p, k], p, 4, 0, k, axis)
                add(acc.at[p, jj, :, half], far1.at[p, k])
                go(acc.at[p, jj, :, half], near1.at[p, k, :, half], p, 4, 0, 4 + k, way, axis)

    issue(0)
    issue(1)
    for jj in range(4):
        middle(jj)
        if jj + 2 < 4:
            issue(jj + 2)
        if jj >= 1:
            finish(jj - 1)
    finish(3)
    for p in parts:
        axis = (p + 1) % 3
        wait_in(near1.at[p, 0, :, bottom], p, 4, 0, 2, axis)
        wait_in(near1.at[p, 1, :, top], p, 4, 0, 3, axis)
        wait_in(near1.at[p, 0, :, top], p, 4, 0, 4, axis)
        wait_in(near1.at[p, 1, :, bottom], p, 4, 0, 5, axis)
        add(acc.at[p, 3], near1.at[p, 0], near1.at[p, 1])
        t = [(me[p] + by + 4) % 4 for by in (2, 1, -1, 0)]
        go(acc.at[p, 3, t[0], top], far2.at[p, 0], p, 5, 0, 0, 1, p)
        go(acc.at[p, 3, t[0], bottom], far2.at[p, 1], p, 5, 0, 1, -1, p)
        go(acc.at[p, 3, t[1], bottom], near2.at[p, 0, bottom], p, 5, 0, 2, 1, p)
        go(acc.at[p, 3, t[2], top], near2.at[p, 1, top], p, 5, 0, 3, -1, p)
    for p in parts:
        t = [(me[p] + by + 4) % 4 for by in (2, 1, -1, 0)]
        for k, way, half in ((0, 1, top), (1, -1, bottom)):
            wait_in(far2.at[p, k], p, 5, 0, k, p)
            own2[p, k] = (
                acc[p, 3, t[1 + k], half].astype(F32) + far2[p, k].astype(F32)
            ).astype(BF16)
            go(own2.at[p, k], near2.at[p, k, half], p, 5, 0, 4 + k, way, p)
    for p in parts:
        wait_in(near2.at[p, 0, bottom], p, 5, 0, 2, p)
        wait_in(near2.at[p, 1, top], p, 5, 0, 3, p)
        wait_in(near2.at[p, 0, top], p, 5, 0, 4, p)
        wait_in(near2.at[p, 1, bottom], p, 5, 0, 5, p)
        out[p] = (
            acc[p, 3, me[p]].astype(F32) + near2[p, 0].astype(F32) + near2[p, 1].astype(F32)
        ).astype(BF16)
    for c in sent:
        c.wait_send()


def scatter(part):
    half = ROWS // 2
    return pl.pallas_call(
        scatter_kernel,
        out_shape=jax.ShapeDtypeStruct((PARTS, ROWS, PW), BF16),
        in_specs=[ANY],
        out_specs=pl.BlockSpec(memory_space=pltpu.VMEM),
        scratch_shapes=[
            pltpu.VMEM((PARTS, 4, 2, 4, half, PW), BF16),
            pltpu.VMEM((PARTS, 4, 2, 4, ROWS, PW), BF16),
            pltpu.VMEM((PARTS, 4, 2, 4, half, PW), BF16),
            pltpu.VMEM((PARTS, 4, 4, ROWS, PW), BF16),
            pltpu.VMEM((PARTS, 2, 4, half, PW), BF16),
            pltpu.VMEM((PARTS, 2, 4, ROWS, PW), BF16),
            pltpu.VMEM((PARTS, 2, half, PW), BF16),
            pltpu.VMEM((PARTS, 2, ROWS, PW), BF16),
            pltpu.VMEM((PARTS, 2, half, PW), BF16),
            pltpu.SemaphoreType.DMA((2, PARTS, 6, 6)),
            pltpu.SemaphoreType.DMA((PARTS, 4, 3)),
        ],
        compiler_params=pltpu.CompilerParams(
            collective_id=2, has_side_effects=True, vmem_limit_bytes=VMEM
        ),
    )(part)


def with_meta(tokens, routes, combine):
    flat = routes.reshape(-1)
    index = jnp.arange(flat.shape[0], dtype=jnp.int32)
    same = (flat[:, None] == flat[None, :]) & (index[None, :] < index[:, None])
    rank = jnp.sum(same.astype(jnp.int32), axis=1).reshape(routes.shape)
    high = lax.reduce_precision(combine, 8, 7)
    rest = combine - high
    middle = lax.reduce_precision(rest, 8, 7)
    low = rest - middle
    named = routes.astype(F32)
    columns = [high, middle, low, jnp.zeros((ROWS, 52), F32), named, named, named]
    columns += [jnp.zeros((ROWS, 4), F32), rank.astype(F32), jnp.zeros((ROWS, 44), F32)]
    meta = jnp.concatenate(columns, axis=1).astype(BF16)
    pad = jnp.zeros((ROWS, PARTS * PW - 128 - D), BF16)
    wide = jnp.concatenate([tokens, pad, meta], axis=1)
    return wide.reshape(ROWS, PARTS, PW).transpose(1, 0, 2)


def local(tokens, routes, combine, gv, gs, uv, us, dv, ds):
    weights = [w.transpose(1, 0, 2) for w in (gv, gs, uv, us, dv, ds)]
    every, ready = gather(with_meta(tokens, routes, combine), *weights)
    hidden, place = upward(every, ready)
    partial = downward(hidden, place, ready)
    result = scatter(partial)
    return result.transpose(1, 0, 2).reshape(ROWS, PARTS * PW)[:, :D]


def solution(mesh):
    rows = P(("eg", "tp"), None)
    weight = P("tp", "eg", None)
    return jax.shard_map(
        local,
        mesh=mesh,
        in_specs=(rows, rows, rows) + (weight,) * 6,
        out_specs=rows,
        check_vma=False,
    )
```

```python
import functools

import jax
import jax.numpy as jnp
from jax import lax
from jax.experimental import pallas as pl
from jax.experimental.pallas import tpu as pltpu
from jax.sharding import PartitionSpec as P

MESH = pl.DeviceIdType.MESH
ANY = pl.BlockSpec(memory_space=pl.ANY)
BF16, F32 = jnp.bfloat16, jnp.float32

D, FS, EXP, ROWS = 2880, 45, 32, 64
PARTS, PW = 3, 1024
FP = 48
META = 896
BLOCK = 32
VMEM = 62 * 1024 * 1024


def position():
    eg, z = lax.axis_index("eg"), lax.axis_index("tp")
    return (eg // 8, (eg // 2) % 4, z), eg % 2


def device(at, core):
    return ((at[0] * 4 + at[1]) * 2 + core, at[2])


def moved(at, axis, by):
    at = list(at)
    at[axis] = (at[axis] + by + 4) % 4
    return tuple(at)


def greet(at, core, sibling):
    barrier = pltpu.get_barrier_semaphore()
    for axis in range(3):
        for way in (1, -1):
            pl.semaphore_signal(
                barrier, inc=1, device_id=device(moved(at, axis, way), core), device_id_type=MESH
            )
    if sibling:
        pl.semaphore_signal(barrier, inc=1, device_id=device(at, 1 - core), device_id_type=MESH)
    pl.semaphore_wait(barrier, 7 if sibling else 6)


WIDE = 512
PIECES = 3 * PARTS * PW // WIDE
PITCH = EXP + 1


def gather_kernel(
    tok, gv, gs, uv, us, dv, ds, every, weights, raw, scales, flat, made, ssem, rsem, lsem, wsem, dsem
):
    me, core = position()
    fetched = []
    for i, (values, scale) in enumerate(((gv, gs), (uv, us), (dv, ds))):
        fetched.append(pltpu.make_async_copy(values, raw.at[i], dsem.at[2 * i]))
        fetched.append(pltpu.make_async_copy(scale, scales.at[i], dsem.at[2 * i + 1]))
    for c in fetched:
        c.start()
    greet(me, core, True)

    def target(n, first):
        start = pl.multiple_of(n // 3 * WIDE, WIDE)
        return weights.at[:, n % 3, pl.ds(first, FP), pl.ds(start, WIDE)]

    def keep(n):
        return pltpu.make_async_copy(made.at[n % 2], target(n, 0), wsem.at[2, n % 2])

    def give(n):
        return pltpu.make_async_remote_copy(
            made.at[n % 2],
            target(n, FP),
            wsem.at[0, n % 2],
            wsem.at[1, n],
            device_id=device(me, 1 - core),
            device_id_type=MESH,
        )

    def dequantize(column, which):
        n = column * 3 + which
        slot = n % 2

        @pl.when(n >= 2)
        def _():
            keep(n - 2).wait()
            give(n - 2).wait_send()

        start = column * WIDE
        real = min(WIDE, D - start)
        blocks = D // BLOCK
        lane = lax.broadcasted_iota(jnp.int32, (blocks, WIDE), 1) + start
        spread = (lane // BLOCK == lax.broadcasted_iota(jnp.int32, (blocks, WIDE), 0)).astype(BF16)
        def units(i, _):
            count = 5
            scale = jnp.dot(
                scales[which, pl.ds(i * count, count)].reshape(count * EXP, blocks),
                spread,
                preferred_element_type=F32,
            )
            values = raw[which, pl.ds(i * count, count), :, pl.ds(start, real)]
            full = values.reshape(count * EXP, real).astype(F32) * scale[:, :real]
            if real < WIDE:
                full = jnp.concatenate([full, jnp.zeros((count * EXP, WIDE - real), F32)], axis=1)
            for c in range(WIDE // 128):
                for k in range(count):
                    flat[c, pl.ds((i * count + k) * PITCH, EXP), :] = full[
                        k * EXP : (k + 1) * EXP, c * 128 : (c + 1) * 128
                    ]
            return 0

        lax.fori_loop(0, FS // 5, units, 0)

        def expert(e, _):
            for c in range(WIDE // 128):
                rows = flat[c, pl.ds(e, FS, stride=PITCH), :]
                rows = jnp.concatenate([rows, jnp.zeros((FP - FS, 128), F32)], axis=0)
                made[slot, e, :, pl.ds(c * 128, 128)] = rows.astype(BF16)
            return 0

        lax.fori_loop(0, EXP, expert, 0, unroll=4)
        keep(n).start()
        give(n).start()

    def work(*columns):
        for column in columns:
            lax.fori_loop(0, 3, lambda which, _: dequantize(column, which) or 0, 0)

    own = [
        pltpu.make_async_copy(tok.at[p], every.at[p, me[0], me[1], me[2]], lsem.at[p])
        for p in range(PARTS)
    ]
    for c in own:
        c.start()

    def region(p, phase, j, source, half):
        order = [p, (p + 1) % 3, (p + 2) % 3]
        index = [slice(None)] * 3
        index[order[phase]] = source
        if phase == 0:
            index[order[1]], index[order[2]] = me[order[1]], me[order[2]]
        elif phase == 1:
            index[order[2]] = me[order[2]]
        else:
            index[order[1]] = j
        rows = slice(None) if half is None else pl.ds(half * 32, 32)
        return every.at[(p, *index, rows)]

    def describe(p, phase, jj, way, step, arriving):
        axis = (p + phase) % 3
        back = way * (step + (1 if arriving else 0))
        source = (me[axis] - back + 8) % 4
        half = None if step == 0 else (0 if way == 1 else 1)
        j = None if phase < 2 else (me[(p + 1) % 3] + (0, -1, 1, 2)[jj] + 4) % 4
        there = region(p, phase, j, source, half)
        here = tok.at[p] if phase == 0 and step == 0 else there
        slot, kind = phase + jj, (0 if way == 1 else 1) + 2 * step
        return pltpu.make_async_remote_copy(
            here,
            there,
            ssem.at[p, slot, kind],
            rsem.at[p, slot, kind],
            device_id=device(moved(me, axis, way), core),
            device_id_type=MESH,
        )

    sent = []

    def go(p, phase, jj, way, step):
        c = describe(p, phase, jj, way, step, False)
        c.start()
        sent.append(c)

    def arrive(p, phase, jj, way, step):
        describe(p, phase, jj, way, step, True).wait_recv()

    parts, ways = range(PARTS), (1, -1)
    for p in parts:
        for way in ways:
            go(p, 0, 0, way, 0)
    for c in fetched:
        c.wait()
    for p in parts:
        for way in ways:
            arrive(p, 0, 0, way, 0)
            go(p, 0, 0, way, 1)
    for c in own:
        c.wait()
    for p in parts:
        for way in ways:
            arrive(p, 0, 0, way, 1)
        for way in ways:
            go(p, 1, 0, way, 0)
    for p in parts:
        for way in ways:
            go(p, 2, 0, way, 0)
    for p in parts:
        for way in ways:
            arrive(p, 1, 0, way, 0)
            go(p, 1, 0, way, 1)
    for p in parts:
        for jj in (1, 2):
            for way in ways:
                go(p, 2, jj, way, 0)
    for p in parts:
        for way in ways:
            arrive(p, 1, 0, way, 1)
        for way in ways:
            go(p, 2, 3, way, 0)
    for jj in range(4):
        work(*((0, 1), (2,), (3,), (4,))[jj])
        for p in parts:
            for way in ways:
                arrive(p, 2, jj, way, 0)
                go(p, 2, jj, way, 1)
    work(5)
    for jj in range(4):
        for p in parts:
            for way in ways:
                arrive(p, 2, jj, way, 1)
    for c in sent:
        c.wait_send()
    for n in (PIECES - 2, PIECES - 1):
        keep(n).wait()
        give(n).wait_send()

    def received(n, _):
        give(n).wait_recv()
        return 0

    lax.fori_loop(0, PIECES, received, 0)


def gather(tok, *weights):
    return pl.pallas_call(
        gather_kernel,
        out_shape=[
            jax.ShapeDtypeStruct((PARTS, 4, 4, 4, ROWS, PW), BF16),
            jax.ShapeDtypeStruct((EXP, 3, 2 * FP, PARTS * PW), BF16),
        ],
        in_specs=[ANY] * 7,
        out_specs=[ANY] * 2,
        scratch_shapes=[
            pltpu.VMEM((3, FS, EXP, D), BF16),
            pltpu.VMEM((3, FS, EXP, D // BLOCK), BF16),
            pltpu.VMEM((WIDE // 128, FS * PITCH, 128), F32),
            pltpu.VMEM((2, EXP, FP, WIDE), BF16),
            pltpu.SemaphoreType.DMA((PARTS, 6, 4)),
            pltpu.SemaphoreType.DMA((PARTS, 6, 4)),
            pltpu.SemaphoreType.DMA((PARTS,)),
            pltpu.SemaphoreType.DMA((3, PIECES)),
            pltpu.SemaphoreType.DMA((6,)),
        ],
        compiler_params=pltpu.CompilerParams(
            collective_id=1, has_side_effects=True, vmem_limit_bytes=VMEM
        ),
    )(tok, *weights)


PER_STEP = 4


def upward_kernel(every, meta, weights, hidden, place, rows, acc):
    p, step = pl.program_id(0), pl.program_id(1)
    z = lax.axis_index("tp")

    @pl.when((p == 0) & (step == 0))
    def _():
        slots = lax.broadcasted_iota(jnp.int32, (ROWS, EXP * 16), 1).astype(F32)

        def block(i, _):
            g, b = i // 4, i % 4
            m = meta[0, g // 4, g % 4, b].astype(F32)
            local = m[:, 64:68] - (z * EXP).astype(F32)
            ids = local * 16.0 + b.astype(F32) * 4.0 + m[:, 80:84]
            ids = jnp.where((local >= 0.0) & (local < EXP), ids, -1.0)
            hit = slots == ids[:, 0:1]
            for k in range(1, 4):
                hit = hit | (slots == ids[:, k : k + 1])
            place[g, pl.ds(b * ROWS, ROWS), :] = hit.astype(F32).astype(BF16)
            return 0

        lax.fori_loop(0, 64, block, 0)

        def clear(e, _):
            acc[e] = jnp.zeros((256, 256), F32)
            return 0

        lax.fori_loop(0, EXP, clear, 0)

    @pl.when(step == 0)
    def _():
        def group(g, _):
            x = every[0, g // 4, g % 4].reshape(4 * ROWS, PW)
            picked = lax.dot_general(
                place[g], x, (((0,), (0,)), ((), ())), preferred_element_type=F32
            )
            rows[:, pl.ds(g * 16, 16), :] = picked.astype(BF16).reshape(EXP, 16, PW)
            return 0

        lax.fori_loop(0, 16, group, 0)

    for i in range(PER_STEP):
        e = step * PER_STEP + i
        acc[e, :, pl.ds(0, 4 * FP)] += lax.dot_general(
            rows[e],
            weights[i].reshape(4 * FP, PW),
            (((1,), (1,)), ((), ())),
            preferred_element_type=F32,
        )

    @pl.when(p == PARTS - 1)
    def _():
        ones = jnp.ones((128, 128), BF16)
        lane = lax.broadcasted_iota(jnp.int32, (256, 128), 1)
        for i in range(PER_STEP):
            e = step * PER_STEP + i
            total = acc[e]
            gate, up = total[:, :128], pltpu.roll(total, 128 - 2 * FP, 1)[:, 128:]
            m = rows[e, :, META:].astype(F32)
            named = pltpu.roll(m, 64, 1) == (z * EXP + e).astype(F32)
            chosen = jnp.where(named & (lane < 12), m, 0.0).astype(BF16)
            weight = jnp.dot(chosen, ones, preferred_element_type=F32)
            value = gate / (1.0 + jnp.exp(-gate)) * up * weight
            hidden[e] = value.astype(BF16)


def upward(every, weights):
    return pl.pallas_call(
        upward_kernel,
        grid=(PARTS, EXP // PER_STEP),
        out_shape=[
            jax.ShapeDtypeStruct((EXP, 256, 128), BF16),
            jax.ShapeDtypeStruct((16, 4 * ROWS, EXP * 16), BF16),
        ],
        in_specs=[
            pl.BlockSpec((1, 4, 4, 4, ROWS, PW), lambda p, s: (p, 0, 0, 0, 0, 0)),
            pl.BlockSpec((1, 4, 4, 4, ROWS, 128), lambda p, s: (2, 0, 0, 0, 0, 7)),
            pl.BlockSpec((PER_STEP, 2, 2 * FP, PW), lambda p, s: (s, 0, 0, p)),
        ],
        out_specs=[
            pl.BlockSpec((EXP, 256, 128), lambda p, s: (0, 0, 0)),
            pl.BlockSpec((16, 4 * ROWS, EXP * 16), lambda p, s: (0, 0, 0)),
        ],
        scratch_shapes=[
            pltpu.VMEM((EXP, 256, PW), BF16),
            pltpu.VMEM((EXP, 256, 256), F32),
        ],
        compiler_params=pltpu.CompilerParams(vmem_limit_bytes=VMEM),
    )(every, every, weights)


CHUNKS = 2
CW = PW // CHUNKS
BATCH = 8
BATCHES = EXP // BATCH
STAGES = 8


def downward_kernel(
    hidden, place, weights, out, part,
    far0, near0, mid0, acc, far1, near1, far2, near2, own2,
    results, stage, wbuf, sems, lsem, wsem, psem,
):
    me, core = position()
    parts = range(PARTS)
    sent = []

    def fetch(n):
        unit = n // BATCHES
        start = pl.multiple_of(unit % PARTS * PW + unit // PARTS * CW, CW)
        first = n % BATCHES * BATCH
        return pltpu.make_async_copy(
            weights.at[pl.ds(first, BATCH), 2, :, pl.ds(start, CW)], wbuf.at[n % 2], wsem.at[n % 2]
        )

    fetch(0).start()
    greet(me, core, False)

    def experts(c, p):
        def batch(s, _):
            n = (c * PARTS + p) * BATCHES + s
            fetch(n).wait()

            @pl.when(n + 1 < CHUNKS * PARTS * BATCHES)
            def _():
                fetch(n + 1).start()

            for i in range(BATCH):
                e = s * BATCH + i
                y = jnp.dot(
                    hidden[e, :, : 2 * FP], wbuf[n % 2, i], preferred_element_type=F32
                )
                first = pl.multiple_of(e * 16, 16)
                results[:, pl.ds(first, 16), :] = y.astype(BF16).reshape(16, 16, CW)
            return 0

        lax.fori_loop(0, BATCHES, batch, 0)

    def combine(c, p):
        def store(g):
            return pltpu.make_async_copy(
                stage.at[g % STAGES], part.at[c, p, g // 4, g % 4], psem.at[g % STAGES]
            )

        def group(g, _):
            @pl.when(g >= STAGES)
            def _():
                store(g - STAGES).wait()

            summed = jnp.dot(place[g], results[g], preferred_element_type=F32)
            stage[g % STAGES] = summed.astype(BF16).reshape(4, ROWS, CW)
            store(g).start()
            return 0

        lax.fori_loop(0, 16, group, 0, unroll=2)

        def stored(g, _):
            store(g).wait()
            return 0

        lax.fori_loop(16 - STAGES, 16, stored, 0)

    def copy(here, there, c, p, phase, kind, way, axis):
        return pltpu.make_async_remote_copy(
            here,
            there,
            sems.at[0, c, p, phase, kind],
            sems.at[1, c, p, phase, kind],
            device_id=device(moved(me, axis, way), core),
            device_id_type=MESH,
        )

    def go(*a):
        c = copy(*a)
        c.start()
        sent.append(c)

    def wait_in(there, c, p, phase, kind, axis):
        copy(there, there, c, p, phase, kind, 1, axis).wait_recv()

    top, bottom, whole = pl.ds(0, 32), pl.ds(32, 32), slice(None)

    def piece(c, p, jj, by, rows):
        o1, o2 = (p + 1) % 3, (p + 2) % 3
        index = [slice(None)] * 3
        index[o1] = (me[o1] + (2, 1, -1, 0)[jj] + 4) % 4
        index[o2] = (me[o2] + by + 4) % 4
        return part.at[(c, p, *index, rows)]

    def load(c, p, jj, k):
        by, rows = ((1, top), (-1, bottom), (0, whole))[k]
        there = acc.at[c, p, jj] if k == 2 else mid0.at[c, p, jj, k]
        return pltpu.make_async_copy(piece(c, p, jj, by, rows), there, lsem.at[c, p, jj, k])

    def issue(c, jj, which=parts):
        for p in which:
            axis = (p + 2) % 3
            go(piece(c, p, jj, 2, top), far0.at[c, p, jj, 0], c, p, jj, 0, 1, axis)
            go(piece(c, p, jj, 2, bottom), far0.at[c, p, jj, 1], c, p, jj, 1, -1, axis)
            for k in range(3):
                load(c, p, jj, k).start()
        for p in which:
            axis = (p + 2) % 3
            go(piece(c, p, jj, 1, bottom), near0.at[c, p, jj, 0, :, bottom], c, p, jj, 2, 1, axis)
            go(piece(c, p, jj, -1, top), near0.at[c, p, jj, 1, :, top], c, p, jj, 3, -1, axis)

    def add(target, *others):
        def one(i, _):
            total = target[i].astype(F32)
            for other in others:
                total = total + other[i].astype(F32)
            target[i] = total.astype(BF16)
            return 0

        lax.fori_loop(0, target.shape[0], one, 0)

    def middle(c, jj):
        for p in parts:
            axis = (p + 2) % 3
            for k, way in ((0, 1), (1, -1)):
                half = top if k == 0 else bottom
                load(c, p, jj, k).wait()
                wait_in(far0.at[c, p, jj, k], c, p, jj, k, axis)
                add(mid0.at[c, p, jj, k], far0.at[c, p, jj, k])
                go(mid0.at[c, p, jj, k], near0.at[c, p, jj, k, :, half], c, p, jj, 4 + k, way, axis)

    def collect(near, c, p, phase, axis, lead):
        for kind, k, half in ((2, 0, bottom), (3, 1, top), (4, 0, top), (5, 1, bottom)):
            wait_in(near.at[(*lead, k, *([whole] if phase < 5 else []), half)], c, p, phase, kind, axis)

    def finish(c, jj):
        for p in parts:
            load(c, p, jj, 2).wait()
            collect(near0, c, p, jj, (p + 2) % 3, (c, p, jj))
            add(acc.at[c, p, jj], near0.at[c, p, jj, 0], near0.at[c, p, jj, 1])
            axis = (p + 1) % 3
            if jj == 0:
                go(acc.at[c, p, 0, :, top], far1.at[c, p, 0], c, p, 4, 0, 1, axis)
                go(acc.at[c, p, 0, :, bottom], far1.at[c, p, 1], c, p, 4, 1, -1, axis)
            elif jj == 1:
                go(acc.at[c, p, 1, :, bottom], near1.at[c, p, 0, :, bottom], c, p, 4, 2, 1, axis)
            elif jj == 2:
                go(acc.at[c, p, 2, :, top], near1.at[c, p, 1, :, top], c, p, 4, 3, -1, axis)
        if jj in (1, 2):
            k, way, half = (0, 1, top) if jj == 1 else (1, -1, bottom)
            for p in parts:
                axis = (p + 1) % 3
                wait_in(far1.at[c, p, k], c, p, 4, k, axis)
                add(acc.at[c, p, jj, :, half], far1.at[c, p, k])
                go(acc.at[c, p, jj, :, half], near1.at[c, p, k, :, half], c, p, 4, 4 + k, way, axis)

    def lines(p):
        return [(me[p] + by + 4) % 4 for by in (2, 1, -1, 0)]

    def last_start(c):
        for p in parts:
            collect(near1, c, p, 4, (p + 1) % 3, (c, p))
            add(acc.at[c, p, 3], near1.at[c, p, 0], near1.at[c, p, 1])
            t = lines(p)
            go(acc.at[c, p, 3, t[0], top], far2.at[c, p, 0], c, p, 5, 0, 1, p)
            go(acc.at[c, p, 3, t[0], bottom], far2.at[c, p, 1], c, p, 5, 1, -1, p)
            go(acc.at[c, p, 3, t[1], bottom], near2.at[c, p, 0, bottom], c, p, 5, 2, 1, p)
            go(acc.at[c, p, 3, t[2], top], near2.at[c, p, 1, top], c, p, 5, 3, -1, p)

    def last_middle(c):
        for p in parts:
            t = lines(p)
            for k, way, half in ((0, 1, top), (1, -1, bottom)):
                wait_in(far2.at[c, p, k], c, p, 5, k, p)
                own2[c, p, k] = (
                    acc[c, p, 3, t[1 + k], half].astype(F32) + far2[c, p, k].astype(F32)
                ).astype(BF16)
                go(own2.at[c, p, k], near2.at[c, p, k, half], c, p, 5, 4 + k, way, p)

    def last_finish(c):
        for p in parts:
            collect(near2, c, p, 5, p, (c, p))
            out[c, p] = (
                acc[c, p, 3, me[p]].astype(F32)
                + near2[c, p, 0].astype(F32)
                + near2[c, p, 1].astype(F32)
            ).astype(BF16)

    for p in parts:
        experts(0, p)
        combine(0, p)
        issue(0, 0, (p,))
        issue(0, 1, (p,))
    experts(1, 0)
    middle(0, 0)
    issue(0, 2)
    combine(1, 0)
    issue(1, 0, (0,))
    middle(0, 1)
    issue(0, 3)
    experts(1, 1)
    finish(0, 0)
    combine(1, 1)
    issue(1, 0, (1,))
    middle(0, 2)
    experts(1, 2)
    finish(0, 1)
    middle(0, 3)
    combine(1, 2)
    issue(1, 0, (2,))
    issue(1, 1)
    finish(0, 2)
    finish(0, 3)
    middle(1, 0)
    issue(1, 2)
    last_start(0)
    middle(1, 1)
    issue(1, 3)
    last_middle(0)
    finish(1, 0)
    middle(1, 2)
    finish(1, 1)
    last_finish(0)
    middle(1, 3)
    finish(1, 2)
    finish(1, 3)
    last_start(1)
    last_middle(1)
    last_finish(1)
    for c in sent:
        c.wait_send()


def downward(hidden, place, weights):
    half = ROWS // 2
    vmem = pl.BlockSpec(memory_space=pltpu.VMEM)
    return pl.pallas_call(
        downward_kernel,
        out_shape=[
            jax.ShapeDtypeStruct((CHUNKS, PARTS, ROWS, CW), BF16),
            jax.ShapeDtypeStruct((CHUNKS, PARTS, 4, 4, 4, ROWS, CW), BF16),
        ],
        in_specs=[vmem, vmem, ANY],
        out_specs=[vmem, ANY],
        scratch_shapes=[
            pltpu.VMEM((CHUNKS, PARTS, 4, 2, 4, half, CW), BF16),
            pltpu.VMEM((CHUNKS, PARTS, 4, 2, 4, ROWS, CW), BF16),
            pltpu.VMEM((CHUNKS, PARTS, 4, 2, 4, half, CW), BF16),
            pltpu.VMEM((CHUNKS, PARTS, 4, 4, ROWS, CW), BF16),
            pltpu.VMEM((CHUNKS, PARTS, 2, 4, half, CW), BF16),
            pltpu.VMEM((CHUNKS, PARTS, 2, 4, ROWS, CW), BF16),
            pltpu.VMEM((CHUNKS, PARTS, 2, half, CW), BF16),
            pltpu.VMEM((CHUNKS, PARTS, 2, ROWS, CW), BF16),
            pltpu.VMEM((CHUNKS, PARTS, 2, half, CW), BF16),
            pltpu.VMEM((16, EXP * 16, CW), BF16),
            pltpu.VMEM((STAGES, 4, ROWS, CW), BF16),
            pltpu.VMEM((2, BATCH, 2 * FP, CW), BF16),
            pltpu.SemaphoreType.DMA((2, CHUNKS, PARTS, 6, 6)),
            pltpu.SemaphoreType.DMA((CHUNKS, PARTS, 4, 3)),
            pltpu.SemaphoreType.DMA((2,)),
            pltpu.SemaphoreType.DMA((STAGES,)),
        ],
        compiler_params=pltpu.CompilerParams(
            collective_id=2, has_side_effects=True, vmem_limit_bytes=VMEM
        ),
    )(hidden, place, weights)


def with_meta(tokens, routes, combine):
    flat = routes.reshape(-1)
    index = jnp.arange(flat.shape[0], dtype=jnp.int32)
    same = (flat[:, None] == flat[None, :]) & (index[None, :] < index[:, None])
    rank = jnp.sum(same.astype(jnp.int32), axis=1).reshape(routes.shape)
    high = lax.reduce_precision(combine, 8, 7)
    rest = combine - high
    middle = lax.reduce_precision(rest, 8, 7)
    low = rest - middle
    named = routes.astype(F32)
    columns = [high, middle, low, jnp.zeros((ROWS, 52), F32), named, named, named]
    columns += [jnp.zeros((ROWS, 4), F32), rank.astype(F32), jnp.zeros((ROWS, 44), F32)]
    meta = jnp.concatenate(columns, axis=1).astype(BF16)
    pad = jnp.zeros((ROWS, PARTS * PW - 128 - D), BF16)
    wide = jnp.concatenate([tokens, pad, meta], axis=1)
    return wide.reshape(ROWS, PARTS, PW).transpose(1, 0, 2)


def local(tokens, routes, combine, gv, gs, uv, us, dv, ds):
    weights = [w.transpose(1, 0, 2) for w in (gv, gs, uv, us, dv, ds)]
    every, ready = gather(with_meta(tokens, routes, combine), *weights)
    hidden, place = upward(every, ready)
    result = downward(hidden, place, ready)[0]
    return result.transpose(2, 1, 0, 3).reshape(ROWS, PARTS * PW)[:, :D]


def solution(mesh):
    rows = P(("eg", "tp"), None)
    weight = P("tp", "eg", None)
    return jax.shard_map(
        local,
        mesh=mesh,
        in_specs=(rows, rows, rows) + (weight,) * 6,
        out_specs=rows,
        check_vma=False,
    )
```

```python
import functools

import jax
import jax.numpy as jnp
from jax import lax
from jax.experimental import pallas as pl
from jax.experimental.pallas import tpu as pltpu
from jax.sharding import PartitionSpec as P

MESH = pl.DeviceIdType.MESH
ANY = pl.BlockSpec(memory_space=pl.ANY)
BF16, F32 = jnp.bfloat16, jnp.float32

D, FS, EXP, ROWS = 2880, 45, 32, 64
PARTS, PW = 3, 1024
FP = 48
META = 896
BLOCK = 32
VMEM = 62 * 1024 * 1024


def position():
    eg, z = lax.axis_index("eg"), lax.axis_index("tp")
    return (eg // 8, (eg // 2) % 4, z), eg % 2


def device(at, core):
    return ((at[0] * 4 + at[1]) * 2 + core, at[2])


def moved(at, axis, by):
    at = list(at)
    at[axis] = (at[axis] + by + 4) % 4
    return tuple(at)


def greet(at, core, sibling):
    barrier = pltpu.get_barrier_semaphore()
    for axis in range(3):
        for way in (1, -1):
            pl.semaphore_signal(
                barrier, inc=1, device_id=device(moved(at, axis, way), core), device_id_type=MESH
            )
    if sibling:
        pl.semaphore_signal(barrier, inc=1, device_id=device(at, 1 - core), device_id_type=MESH)
    pl.semaphore_wait(barrier, 7 if sibling else 6)


WIDE = 512
PIECES = 3 * PARTS * PW // WIDE
PITCH = EXP + 1


def gather_kernel(
    tok, gv, gs, uv, us, dv, ds, every, weights, raw, scales, flat, made, ssem, rsem, lsem, wsem, dsem
):
    me, core = position()
    fetched = []
    for i, (values, scale) in enumerate(((gv, gs), (uv, us), (dv, ds))):
        fetched.append(pltpu.make_async_copy(values, raw.at[i], dsem.at[2 * i]))
        fetched.append(pltpu.make_async_copy(scale, scales.at[i], dsem.at[2 * i + 1]))
    for c in fetched:
        c.start()
    greet(me, core, True)

    def target(n, first):
        start = pl.multiple_of(n // 3 * WIDE, WIDE)
        return weights.at[:, n % 3, pl.ds(first, FP), pl.ds(start, WIDE)]

    def keep(n):
        return pltpu.make_async_copy(made.at[n % 2], target(n, 0), wsem.at[2, n % 2])

    def give(n):
        return pltpu.make_async_remote_copy(
            made.at[n % 2],
            target(n, FP),
            wsem.at[0, n % 2],
            wsem.at[1, n],
            device_id=device(me, 1 - core),
            device_id_type=MESH,
        )

    def dequantize(column, which):
        n = column * 3 + which
        slot = n % 2

        @pl.when(n >= 2)
        def _():
            keep(n - 2).wait()
            give(n - 2).wait_send()

        start = column * WIDE
        real = min(WIDE, D - start)
        blocks = D // BLOCK
        lane = lax.broadcasted_iota(jnp.int32, (blocks, WIDE), 1) + start
        spread = (lane // BLOCK == lax.broadcasted_iota(jnp.int32, (blocks, WIDE), 0)).astype(BF16)
        def units(i, _):
            count = 5
            scale = jnp.dot(
                scales[which, pl.ds(i * count, count)].reshape(count * EXP, blocks),
                spread,
                preferred_element_type=F32,
            )
            values = raw[which, pl.ds(i * count, count), :, pl.ds(start, real)]
            full = values.reshape(count * EXP, real).astype(F32) * scale[:, :real]
            if real < WIDE:
                full = jnp.concatenate([full, jnp.zeros((count * EXP, WIDE - real), F32)], axis=1)
            for c in range(WIDE // 128):
                for k in range(count):
                    flat[c, pl.ds((i * count + k) * PITCH, EXP), :] = full[
                        k * EXP : (k + 1) * EXP, c * 128 : (c + 1) * 128
                    ]
            return 0

        lax.fori_loop(0, FS // 5, units, 0)

        def expert(e, _):
            for c in range(WIDE // 128):
                rows = flat[c, pl.ds(e, FS, stride=PITCH), :]
                rows = jnp.concatenate([rows, jnp.zeros((FP - FS, 128), F32)], axis=0)
                made[slot, e, :, pl.ds(c * 128, 128)] = rows.astype(BF16)
            return 0

        lax.fori_loop(0, EXP, expert, 0, unroll=4)
        keep(n).start()
        give(n).start()

    def work(*columns):
        for column in columns:
            lax.fori_loop(0, 3, lambda which, _: dequantize(column, which) or 0, 0)

    own = [
        pltpu.make_async_copy(tok.at[p], every.at[p, me[0], me[1], me[2]], lsem.at[p])
        for p in range(PARTS)
    ]
    for c in own:
        c.start()

    def region(p, phase, j, source, half):
        order = [p, (p + 1) % 3, (p + 2) % 3]
        index = [slice(None)] * 3
        index[order[phase]] = source
        if phase == 0:
            index[order[1]], index[order[2]] = me[order[1]], me[order[2]]
        elif phase == 1:
            index[order[2]] = me[order[2]]
        else:
            index[order[1]] = j
        rows = slice(None) if half is None else pl.ds(half * 32, 32)
        return every.at[(p, *index, rows)]

    def describe(p, phase, jj, way, step, arriving):
        axis = (p + phase) % 3
        back = way * (step + (1 if arriving else 0))
        source = (me[axis] - back + 8) % 4
        half = None if step == 0 else (0 if way == 1 else 1)
        j = None if phase < 2 else (me[(p + 1) % 3] + (0, -1, 1, 2)[jj] + 4) % 4
        there = region(p, phase, j, source, half)
        here = tok.at[p] if phase == 0 and step == 0 else there
        slot, kind = phase + jj, (0 if way == 1 else 1) + 2 * step
        return pltpu.make_async_remote_copy(
            here,
            there,
            ssem.at[p, slot, kind],
            rsem.at[p, slot, kind],
            device_id=device(moved(me, axis, way), core),
            device_id_type=MESH,
        )

    sent = []

    def go(p, phase, jj, way, step):
        c = describe(p, phase, jj, way, step, False)
        c.start()
        sent.append(c)

    def arrive(p, phase, jj, way, step):
        describe(p, phase, jj, way, step, True).wait_recv()

    parts, ways = range(PARTS), (1, -1)
    for p in parts:
        for way in ways:
            go(p, 0, 0, way, 0)
    for c in fetched:
        c.wait()
    for p in parts:
        for way in ways:
            arrive(p, 0, 0, way, 0)
            go(p, 0, 0, way, 1)
    for c in own:
        c.wait()
    for p in parts:
        for way in ways:
            arrive(p, 0, 0, way, 1)
        for way in ways:
            go(p, 1, 0, way, 0)
    for p in parts:
        for way in ways:
            go(p, 2, 0, way, 0)
    for p in parts:
        for way in ways:
            arrive(p, 1, 0, way, 0)
            go(p, 1, 0, way, 1)
    for p in parts:
        for jj in (1, 2):
            for way in ways:
                go(p, 2, jj, way, 0)
    for p in parts:
        for way in ways:
            arrive(p, 1, 0, way, 1)
        for way in ways:
            go(p, 2, 3, way, 0)
    for jj in range(4):
        work(*((0, 1), (2,), (3,), (4,))[jj])
        for p in parts:
            for way in ways:
                arrive(p, 2, jj, way, 0)
                go(p, 2, jj, way, 1)
    work(5)
    for jj in range(4):
        for p in parts:
            for way in ways:
                arrive(p, 2, jj, way, 1)
    for c in sent:
        c.wait_send()
    for n in (PIECES - 2, PIECES - 1):
        keep(n).wait()
        give(n).wait_send()

    def received(n, _):
        give(n).wait_recv()
        return 0

    lax.fori_loop(0, PIECES, received, 0)


def gather(tok, *weights):
    return pl.pallas_call(
        gather_kernel,
        out_shape=[
            jax.ShapeDtypeStruct((PARTS, 4, 4, 4, ROWS, PW), BF16),
            jax.ShapeDtypeStruct((EXP, 3, 2 * FP, PARTS * PW), BF16),
        ],
        in_specs=[ANY] * 7,
        out_specs=[ANY] * 2,
        scratch_shapes=[
            pltpu.VMEM((3, FS, EXP, D), BF16),
            pltpu.VMEM((3, FS, EXP, D // BLOCK), BF16),
            pltpu.VMEM((WIDE // 128, FS * PITCH, 128), F32),
            pltpu.VMEM((2, EXP, FP, WIDE), BF16),
            pltpu.SemaphoreType.DMA((PARTS, 6, 4)),
            pltpu.SemaphoreType.DMA((PARTS, 6, 4)),
            pltpu.SemaphoreType.DMA((PARTS,)),
            pltpu.SemaphoreType.DMA((3, PIECES)),
            pltpu.SemaphoreType.DMA((6,)),
        ],
        compiler_params=pltpu.CompilerParams(
            collective_id=1, has_side_effects=True, vmem_limit_bytes=VMEM
        ),
    )(tok, *weights)


PER_STEP = 4


def upward_kernel(every, meta, weights, hidden, place, rows, acc):
    p, step = pl.program_id(0), pl.program_id(1)
    z = lax.axis_index("tp")

    @pl.when((p == 0) & (step == 0))
    def _():
        slots = lax.broadcasted_iota(jnp.int32, (ROWS, EXP * 16), 1).astype(F32)

        def block(i, _):
            g, b = i // 4, i % 4
            m = meta[0, g // 4, g % 4, b].astype(F32)
            local = m[:, 64:68] - (z * EXP).astype(F32)
            ids = local * 16.0 + b.astype(F32) * 4.0 + m[:, 80:84]
            ids = jnp.where((local >= 0.0) & (local < EXP), ids, -1.0)
            hit = slots == ids[:, 0:1]
            for k in range(1, 4):
                hit = hit | (slots == ids[:, k : k + 1])
            place[g, pl.ds(b * ROWS, ROWS), :] = hit.astype(F32).astype(BF16)
            return 0

        lax.fori_loop(0, 64, block, 0, unroll=4)

        def clear(e, _):
            acc[e] = jnp.zeros((256, 256), F32)
            return 0

        lax.fori_loop(0, EXP, clear, 0)

    @pl.when(step == 0)
    def _():
        def group(g, _):
            x = every[0, g // 4, g % 4].reshape(4 * ROWS, PW)
            picked = lax.dot_general(
                place[g], x, (((0,), (0,)), ((), ())), preferred_element_type=F32
            )
            rows[:, pl.ds(g * 16, 16), :] = picked.astype(BF16).reshape(EXP, 16, PW)
            return 0

        lax.fori_loop(0, 16, group, 0, unroll=2)

    for i in range(PER_STEP):
        e = step * PER_STEP + i
        acc[e, :, pl.ds(0, 4 * FP)] += lax.dot_general(
            rows[e],
            weights[i].reshape(4 * FP, PW),
            (((1,), (1,)), ((), ())),
            preferred_element_type=F32,
        )

    @pl.when(p == PARTS - 1)
    def _():
        ones = jnp.ones((128, 128), BF16)
        lane = lax.broadcasted_iota(jnp.int32, (256, 128), 1)
        for i in range(PER_STEP):
            e = step * PER_STEP + i
            total = acc[e]
            gate, up = total[:, :128], pltpu.roll(total, 128 - 2 * FP, 1)[:, 128:]
            m = rows[e, :, META:].astype(F32)
            named = pltpu.roll(m, 64, 1) == (z * EXP + e).astype(F32)
            chosen = jnp.where(named & (lane < 12), m, 0.0).astype(BF16)
            weight = jnp.dot(chosen, ones, preferred_element_type=F32)
            value = gate / (1.0 + jnp.exp(-gate)) * up * weight
            hidden[e] = value.astype(BF16)


def upward(every, weights):
    return pl.pallas_call(
        upward_kernel,
        grid=(PARTS, EXP // PER_STEP),
        out_shape=[
            jax.ShapeDtypeStruct((EXP, 256, 128), BF16),
            jax.ShapeDtypeStruct((16, 4 * ROWS, EXP * 16), BF16),
        ],
        in_specs=[
            pl.BlockSpec((1, 4, 4, 4, ROWS, PW), lambda p, s: (p, 0, 0, 0, 0, 0)),
            pl.BlockSpec((1, 4, 4, 4, ROWS, 128), lambda p, s: (2, 0, 0, 0, 0, 7)),
            pl.BlockSpec((PER_STEP, 2, 2 * FP, PW), lambda p, s: (s, 0, 0, p)),
        ],
        out_specs=[
            pl.BlockSpec((EXP, 256, 128), lambda p, s: (0, 0, 0)),
            pl.BlockSpec((16, 4 * ROWS, EXP * 16), lambda p, s: (0, 0, 0)),
        ],
        scratch_shapes=[
            pltpu.VMEM((EXP, 256, PW), BF16),
            pltpu.VMEM((EXP, 256, 256), F32),
        ],
        compiler_params=pltpu.CompilerParams(vmem_limit_bytes=VMEM),
    )(every, every, weights)


CHUNKS = 2
CW = PW // CHUNKS
BATCH = 8
BATCHES = EXP // BATCH
STAGES = 8


def downward_kernel(
    hidden, place, weights, out, part,
    far0, near0, mid0, acc, far1, near1, far2, near2, own2,
    results, stage, wbuf, sems, lsem, wsem, psem,
):
    me, core = position()
    parts = range(PARTS)
    sent = []

    def fetch(n):
        unit = n // BATCHES
        start = pl.multiple_of(unit % PARTS * PW + unit // PARTS * CW, CW)
        first = n % BATCHES * BATCH
        return pltpu.make_async_copy(
            weights.at[pl.ds(first, BATCH), 2, :, pl.ds(start, CW)], wbuf.at[n % 2], wsem.at[n % 2]
        )

    fetch(0).start()
    greet(me, core, False)

    def experts(c, p):
        def batch(s, _):
            n = (c * PARTS + p) * BATCHES + s
            fetch(n).wait()

            @pl.when(n + 1 < CHUNKS * PARTS * BATCHES)
            def _():
                fetch(n + 1).start()

            for i in range(BATCH):
                e = s * BATCH + i
                y = jnp.dot(
                    hidden[e, :, : 2 * FP], wbuf[n % 2, i], preferred_element_type=F32
                )
                first = pl.multiple_of(e * 16, 16)
                results[:, pl.ds(first, 16), :] = y.astype(BF16).reshape(16, 16, CW)
            return 0

        lax.fori_loop(0, BATCHES, batch, 0)

    def combine(c, p):
        def store(g):
            return pltpu.make_async_copy(
                stage.at[g % STAGES], part.at[c, p, g // 4, g % 4], psem.at[g % STAGES]
            )

        def group(g, _):
            @pl.when(g >= STAGES)
            def _():
                store(g - STAGES).wait()

            summed = jnp.dot(place[g], results[g], preferred_element_type=F32)
            stage[g % STAGES] = summed.astype(BF16).reshape(4, ROWS, CW)
            store(g).start()
            return 0

        lax.fori_loop(0, 16, group, 0, unroll=2)

        def stored(g, _):
            store(g).wait()
            return 0

        lax.fori_loop(16 - STAGES, 16, stored, 0)

    def copy(here, there, c, p, phase, kind, way, axis):
        return pltpu.make_async_remote_copy(
            here,
            there,
            sems.at[0, c, p, phase, kind],
            sems.at[1, c, p, phase, kind],
            device_id=device(moved(me, axis, way), core),
            device_id_type=MESH,
        )

    def go(*a):
        c = copy(*a)
        c.start()
        sent.append(c)

    def wait_in(there, c, p, phase, kind, axis):
        copy(there, there, c, p, phase, kind, 1, axis).wait_recv()

    top, bottom, whole = pl.ds(0, 32), pl.ds(32, 32), slice(None)

    def piece(c, p, jj, by, rows):
        o1, o2 = (p + 1) % 3, (p + 2) % 3
        index = [slice(None)] * 3
        index[o1] = (me[o1] + (2, 1, -1, 0)[jj] + 4) % 4
        index[o2] = (me[o2] + by + 4) % 4
        return part.at[(c, p, *index, rows)]

    def load(c, p, jj, k):
        by, rows = ((1, top), (-1, bottom), (0, whole))[k]
        there = acc.at[c, p, jj] if k == 2 else mid0.at[c, p, jj, k]
        return pltpu.make_async_copy(piece(c, p, jj, by, rows), there, lsem.at[c, p, jj, k])

    def issue(c, jj, which=parts):
        for p in which:
            axis = (p + 2) % 3
            go(piece(c, p, jj, 2, top), far0.at[c, p, jj, 0], c, p, jj, 0, 1, axis)
            go(piece(c, p, jj, 2, bottom), far0.at[c, p, jj, 1], c, p, jj, 1, -1, axis)
            for k in range(3):
                load(c, p, jj, k).start()
        for p in which:
            axis = (p + 2) % 3
            go(piece(c, p, jj, 1, bottom), near0.at[c, p, jj, 0, :, bottom], c, p, jj, 2, 1, axis)
            go(piece(c, p, jj, -1, top), near0.at[c, p, jj, 1, :, top], c, p, jj, 3, -1, axis)

    def add(target, *others):
        def one(i, _):
            total = target[i].astype(F32)
            for other in others:
                total = total + other[i].astype(F32)
            target[i] = total.astype(BF16)
            return 0

        lax.fori_loop(0, target.shape[0], one, 0)

    def middle(c, jj):
        for p in parts:
            axis = (p + 2) % 3
            for k, way in ((0, 1), (1, -1)):
                half = top if k == 0 else bottom
                load(c, p, jj, k).wait()
                wait_in(far0.at[c, p, jj, k], c, p, jj, k, axis)
                add(mid0.at[c, p, jj, k], far0.at[c, p, jj, k])
                go(mid0.at[c, p, jj, k], near0.at[c, p, jj, k, :, half], c, p, jj, 4 + k, way, axis)

    def collect(near, c, p, phase, axis, lead):
        for kind, k, half in ((2, 0, bottom), (3, 1, top), (4, 0, top), (5, 1, bottom)):
            wait_in(near.at[(*lead, k, *([whole] if phase < 5 else []), half)], c, p, phase, kind, axis)

    def finish(c, jj):
        for p in parts:
            load(c, p, jj, 2).wait()
            collect(near0, c, p, jj, (p + 2) % 3, (c, p, jj))
            add(acc.at[c, p, jj], near0.at[c, p, jj, 0], near0.at[c, p, jj, 1])
            axis = (p + 1) % 3
            if jj == 0:
                go(acc.at[c, p, 0, :, top], far1.at[c, p, 0], c, p, 4, 0, 1, axis)
                go(acc.at[c, p, 0, :, bottom], far1.at[c, p, 1], c, p, 4, 1, -1, axis)
            elif jj == 1:
                go(acc.at[c, p, 1, :, bottom], near1.at[c, p, 0, :, bottom], c, p, 4, 2, 1, axis)
            elif jj == 2:
                go(acc.at[c, p, 2, :, top], near1.at[c, p, 1, :, top], c, p, 4, 3, -1, axis)
        if jj in (1, 2):
            k, way, half = (0, 1, top) if jj == 1 else (1, -1, bottom)
            for p in parts:
                axis = (p + 1) % 3
                wait_in(far1.at[c, p, k], c, p, 4, k, axis)
                add(acc.at[c, p, jj, :, half], far1.at[c, p, k])
                go(acc.at[c, p, jj, :, half], near1.at[c, p, k, :, half], c, p, 4, 4 + k, way, axis)

    def lines(p):
        return [(me[p] + by + 4) % 4 for by in (2, 1, -1, 0)]

    def last_start(c):
        for p in parts:
            collect(near1, c, p, 4, (p + 1) % 3, (c, p))
            add(acc.at[c, p, 3], near1.at[c, p, 0], near1.at[c, p, 1])
            t = lines(p)
            go(acc.at[c, p, 3, t[0], top], far2.at[c, p, 0], c, p, 5, 0, 1, p)
            go(acc.at[c, p, 3, t[0], bottom], far2.at[c, p, 1], c, p, 5, 1, -1, p)
            go(acc.at[c, p, 3, t[1], bottom], near2.at[c, p, 0, bottom], c, p, 5, 2, 1, p)
            go(acc.at[c, p, 3, t[2], top], near2.at[c, p, 1, top], c, p, 5, 3, -1, p)

    def last_middle(c):
        for p in parts:
            t = lines(p)
            for k, way, half in ((0, 1, top), (1, -1, bottom)):
                wait_in(far2.at[c, p, k], c, p, 5, k, p)
                own2[c, p, k] = (
                    acc[c, p, 3, t[1 + k], half].astype(F32) + far2[c, p, k].astype(F32)
                ).astype(BF16)
                go(own2.at[c, p, k], near2.at[c, p, k, half], c, p, 5, 4 + k, way, p)

    def last_finish(c):
        for p in parts:
            collect(near2, c, p, 5, p, (c, p))
            out[c, p] = (
                acc[c, p, 3, me[p]].astype(F32)
                + near2[c, p, 0].astype(F32)
                + near2[c, p, 1].astype(F32)
            ).astype(BF16)

    for p in parts:
        experts(0, p)
        combine(0, p)
        issue(0, 0, (p,))
        issue(0, 1, (p,))
    experts(1, 0)
    middle(0, 0)
    issue(0, 2)
    combine(1, 0)
    issue(1, 0, (0,))
    middle(0, 1)
    issue(0, 3)
    experts(1, 1)
    finish(0, 0)
    combine(1, 1)
    issue(1, 0, (1,))
    middle(0, 2)
    experts(1, 2)
    finish(0, 1)
    middle(0, 3)
    combine(1, 2)
    issue(1, 0, (2,))
    issue(1, 1)
    finish(0, 2)
    finish(0, 3)
    middle(1, 0)
    issue(1, 2)
    last_start(0)
    middle(1, 1)
    issue(1, 3)
    last_middle(0)
    finish(1, 0)
    middle(1, 2)
    finish(1, 1)
    last_finish(0)
    middle(1, 3)
    finish(1, 2)
    finish(1, 3)
    last_start(1)
    last_middle(1)
    last_finish(1)
    for c in sent:
        c.wait_send()


def downward(hidden, place, weights):
    half = ROWS // 2
    vmem = pl.BlockSpec(memory_space=pltpu.VMEM)
    return pl.pallas_call(
        downward_kernel,
        out_shape=[
            jax.ShapeDtypeStruct((CHUNKS, PARTS, ROWS, CW), BF16),
            jax.ShapeDtypeStruct((CHUNKS, PARTS, 4, 4, 4, ROWS, CW), BF16),
        ],
        in_specs=[vmem, vmem, ANY],
        out_specs=[vmem, ANY],
        scratch_shapes=[
            pltpu.VMEM((CHUNKS, PARTS, 4, 2, 4, half, CW), BF16),
            pltpu.VMEM((CHUNKS, PARTS, 4, 2, 4, ROWS, CW), BF16),
            pltpu.VMEM((CHUNKS, PARTS, 4, 2, 4, half, CW), BF16),
            pltpu.VMEM((CHUNKS, PARTS, 4, 4, ROWS, CW), BF16),
            pltpu.VMEM((CHUNKS, PARTS, 2, 4, half, CW), BF16),
            pltpu.VMEM((CHUNKS, PARTS, 2, 4, ROWS, CW), BF16),
            pltpu.VMEM((CHUNKS, PARTS, 2, half, CW), BF16),
            pltpu.VMEM((CHUNKS, PARTS, 2, ROWS, CW), BF16),
            pltpu.VMEM((CHUNKS, PARTS, 2, half, CW), BF16),
            pltpu.VMEM((16, EXP * 16, CW), BF16),
            pltpu.VMEM((STAGES, 4, ROWS, CW), BF16),
            pltpu.VMEM((2, BATCH, 2 * FP, CW), BF16),
            pltpu.SemaphoreType.DMA((2, CHUNKS, PARTS, 6, 6)),
            pltpu.SemaphoreType.DMA((CHUNKS, PARTS, 4, 3)),
            pltpu.SemaphoreType.DMA((2,)),
            pltpu.SemaphoreType.DMA((STAGES,)),
        ],
        compiler_params=pltpu.CompilerParams(
            collective_id=2, has_side_effects=True, vmem_limit_bytes=VMEM
        ),
    )(hidden, place, weights)


def with_meta(tokens, routes, combine):
    flat = routes.reshape(-1)
    index = jnp.arange(flat.shape[0], dtype=jnp.int32)
    same = (flat[:, None] == flat[None, :]) & (index[None, :] < index[:, None])
    rank = jnp.sum(same.astype(jnp.int32), axis=1).reshape(routes.shape)
    high = lax.reduce_precision(combine, 8, 7)
    rest = combine - high
    middle = lax.reduce_precision(rest, 8, 7)
    low = rest - middle
    named = routes.astype(F32)
    columns = [high, middle, low, jnp.zeros((ROWS, 52), F32), named, named, named]
    columns += [jnp.zeros((ROWS, 4), F32), rank.astype(F32), jnp.zeros((ROWS, 44), F32)]
    meta = jnp.concatenate(columns, axis=1).astype(BF16)
    pad = jnp.zeros((ROWS, PARTS * PW - 128 - D), BF16)
    wide = jnp.concatenate([tokens, pad, meta], axis=1)
    return wide.reshape(ROWS, PARTS, PW).transpose(1, 0, 2)


def local(tokens, routes, combine, gv, gs, uv, us, dv, ds):
    weights = [w.transpose(1, 0, 2) for w in (gv, gs, uv, us, dv, ds)]
    every, ready = gather(with_meta(tokens, routes, combine), *weights)
    hidden, place = upward(every, ready)
    result = downward(hidden, place, ready)[0]
    return result.transpose(2, 1, 0, 3).reshape(ROWS, PARTS * PW)[:, :D]


def solution(mesh):
    rows = P(("eg", "tp"), None)
    weight = P("tp", "eg", None)
    return jax.shard_map(
        local,
        mesh=mesh,
        in_specs=(rows, rows, rows) + (weight,) * 6,
        out_specs=rows,
        check_vma=False,
    )
```

```python
import functools

import jax
import jax.numpy as jnp
from jax import lax
from jax.experimental import pallas as pl
from jax.experimental.pallas import tpu as pltpu
from jax.sharding import PartitionSpec as P

MESH = pl.DeviceIdType.MESH
ANY = pl.BlockSpec(memory_space=pl.ANY)
BF16, F32 = jnp.bfloat16, jnp.float32

D, FS, EXP, ROWS = 2880, 45, 32, 64
PARTS, PW = 3, 1024
FP = 48
META = 896
BLOCK = 32
VMEM = 62 * 1024 * 1024


def position():
    eg, z = lax.axis_index("eg"), lax.axis_index("tp")
    return (eg // 8, (eg // 2) % 4, z), eg % 2


def device(at, core):
    return ((at[0] * 4 + at[1]) * 2 + core, at[2])


def moved(at, axis, by):
    at = list(at)
    at[axis] = (at[axis] + by + 4) % 4
    return tuple(at)


def greet(at, core, sibling):
    barrier = pltpu.get_barrier_semaphore()
    for axis in range(3):
        for way in (1, -1):
            pl.semaphore_signal(
                barrier, inc=1, device_id=device(moved(at, axis, way), core), device_id_type=MESH
            )
    if sibling:
        pl.semaphore_signal(barrier, inc=1, device_id=device(at, 1 - core), device_id_type=MESH)
    pl.semaphore_wait(barrier, 7 if sibling else 6)


WIDE = 512
PIECES = 3 * PARTS * PW // WIDE
PITCH = EXP + 1


def gather_kernel(
    tok, gv, gs, uv, us, dv, ds, every, weights, raw, scales, flat, made, ssem, rsem, lsem, wsem, dsem
):
    me, core = position()
    fetched = []
    for i, (values, scale) in enumerate(((gv, gs), (uv, us), (dv, ds))):
        fetched.append(pltpu.make_async_copy(values, raw.at[i], dsem.at[2 * i]))
        fetched.append(pltpu.make_async_copy(scale, scales.at[i], dsem.at[2 * i + 1]))
    for c in fetched:
        c.start()
    greet(me, core, True)

    def target(n, first):
        start = pl.multiple_of(n // 3 * WIDE, WIDE)
        return weights.at[:, n % 3, pl.ds(first, FP), pl.ds(start, WIDE)]

    def keep(n):
        return pltpu.make_async_copy(made.at[n % 2], target(n, 0), wsem.at[2, n % 2])

    def give(n):
        return pltpu.make_async_remote_copy(
            made.at[n % 2],
            target(n, FP),
            wsem.at[0, n % 2],
            wsem.at[1, n],
            device_id=device(me, 1 - core),
            device_id_type=MESH,
        )

    def dequantize(column, which):
        n = column * 3 + which
        slot = n % 2

        @pl.when(n >= 2)
        def _():
            keep(n - 2).wait()
            give(n - 2).wait_send()

        start = column * WIDE
        real = min(WIDE, D - start)
        blocks = D // BLOCK
        lane = lax.broadcasted_iota(jnp.int32, (blocks, WIDE), 1) + start
        spread = (lane // BLOCK == lax.broadcasted_iota(jnp.int32, (blocks, WIDE), 0)).astype(BF16)
        def units(i, _):
            count = 5
            scale = jnp.dot(
                scales[which, pl.ds(i * count, count)].reshape(count * EXP, blocks),
                spread,
                preferred_element_type=F32,
            )
            values = raw[which, pl.ds(i * count, count), :, pl.ds(start, real)]
            full = values.reshape(count * EXP, real).astype(F32) * scale[:, :real]
            if real < WIDE:
                full = jnp.concatenate([full, jnp.zeros((count * EXP, WIDE - real), F32)], axis=1)
            for c in range(WIDE // 128):
                for k in range(count):
                    flat[c, pl.ds((i * count + k) * PITCH, EXP), :] = full[
                        k * EXP : (k + 1) * EXP, c * 128 : (c + 1) * 128
                    ]
            return 0

        lax.fori_loop(0, FS // 5, units, 0)

        def expert(e, _):
            for c in range(WIDE // 128):
                rows = flat[c, pl.ds(e, FS, stride=PITCH), :]
                rows = jnp.concatenate([rows, jnp.zeros((FP - FS, 128), F32)], axis=0)
                made[slot, e, :, pl.ds(c * 128, 128)] = rows.astype(BF16)
            return 0

        lax.fori_loop(0, EXP, expert, 0, unroll=4)
        keep(n).start()
        give(n).start()

    def work(*columns):
        for column in columns:
            lax.fori_loop(0, 3, lambda which, _: dequantize(column, which) or 0, 0)

    own = [
        pltpu.make_async_copy(tok.at[p], every.at[p, me[0], me[1], me[2]], lsem.at[p])
        for p in range(PARTS)
    ]
    for c in own:
        c.start()

    def region(p, phase, j, source, half):
        order = [p, (p + 1) % 3, (p + 2) % 3]
        index = [slice(None)] * 3
        index[order[phase]] = source
        if phase == 0:
            index[order[1]], index[order[2]] = me[order[1]], me[order[2]]
        elif phase == 1:
            index[order[2]] = me[order[2]]
        else:
            index[order[1]] = j
        rows = slice(None) if half is None else pl.ds(half * 32, 32)
        return every.at[(p, *index, rows)]

    def describe(p, phase, jj, way, step, arriving):
        axis = (p + phase) % 3
        back = way * (step + (1 if arriving else 0))
        source = (me[axis] - back + 8) % 4
        half = None if step == 0 else (0 if way == 1 else 1)
        j = None if phase < 2 else (me[(p + 1) % 3] + (0, -1, 1, 2)[jj] + 4) % 4
        there = region(p, phase, j, source, half)
        here = tok.at[p] if phase == 0 and step == 0 else there
        slot, kind = phase + jj, (0 if way == 1 else 1) + 2 * step
        return pltpu.make_async_remote_copy(
            here,
            there,
            ssem.at[p, slot, kind],
            rsem.at[p, slot, kind],
            device_id=device(moved(me, axis, way), core),
            device_id_type=MESH,
        )

    sent = []

    def go(p, phase, jj, way, step):
        c = describe(p, phase, jj, way, step, False)
        c.start()
        sent.append(c)

    def arrive(p, phase, jj, way, step):
        describe(p, phase, jj, way, step, True).wait_recv()

    parts, ways = range(PARTS), (1, -1)
    for p in parts:
        for way in ways:
            go(p, 0, 0, way, 0)
    for c in fetched:
        c.wait()
    for p in parts:
        for way in ways:
            arrive(p, 0, 0, way, 0)
            go(p, 0, 0, way, 1)
    for c in own:
        c.wait()
    for p in parts:
        for way in ways:
            arrive(p, 0, 0, way, 1)
        for way in ways:
            go(p, 1, 0, way, 0)
    for p in parts:
        for way in ways:
            go(p, 2, 0, way, 0)
    for p in parts:
        for way in ways:
            arrive(p, 1, 0, way, 0)
            go(p, 1, 0, way, 1)
    for p in parts:
        for jj in (1, 2):
            for way in ways:
                go(p, 2, jj, way, 0)
    for p in parts:
        for way in ways:
            arrive(p, 1, 0, way, 1)
        for way in ways:
            go(p, 2, 3, way, 0)
    for jj in range(4):
        work(*((0, 1), (2,), (3,), (4,))[jj])
        for p in parts:
            for way in ways:
                arrive(p, 2, jj, way, 0)
                go(p, 2, jj, way, 1)
    work(5)
    for jj in range(4):
        for p in parts:
            for way in ways:
                arrive(p, 2, jj, way, 1)
    for c in sent:
        c.wait_send()
    for n in (PIECES - 2, PIECES - 1):
        keep(n).wait()
        give(n).wait_send()

    def received(n, _):
        give(n).wait_recv()
        return 0

    lax.fori_loop(0, PIECES, received, 0)


def gather(tok, *weights):
    return pl.pallas_call(
        gather_kernel,
        out_shape=[
            jax.ShapeDtypeStruct((PARTS, 4, 4, 4, ROWS, PW), BF16),
            jax.ShapeDtypeStruct((EXP, 3, 2 * FP, PARTS * PW), BF16),
        ],
        in_specs=[ANY] * 7,
        out_specs=[ANY] * 2,
        scratch_shapes=[
            pltpu.VMEM((3, FS, EXP, D), BF16),
            pltpu.VMEM((3, FS, EXP, D // BLOCK), BF16),
            pltpu.VMEM((WIDE // 128, FS * PITCH, 128), F32),
            pltpu.VMEM((2, EXP, FP, WIDE), BF16),
            pltpu.SemaphoreType.DMA((PARTS, 6, 4)),
            pltpu.SemaphoreType.DMA((PARTS, 6, 4)),
            pltpu.SemaphoreType.DMA((PARTS,)),
            pltpu.SemaphoreType.DMA((3, PIECES)),
            pltpu.SemaphoreType.DMA((6,)),
        ],
        compiler_params=pltpu.CompilerParams(
            collective_id=1, has_side_effects=True, vmem_limit_bytes=VMEM
        ),
    )(tok, *weights)


PER_STEP = 4


def upward_kernel(every, meta, weights, hidden, place, rows, acc):
    p, step = pl.program_id(0), pl.program_id(1)
    z = lax.axis_index("tp")

    @pl.when((p == 0) & (step == 0))
    def _():
        slots = lax.broadcasted_iota(jnp.int32, (ROWS, EXP * 16), 1).astype(F32)

        def block(i, _):
            g, b = i // 4, i % 4
            m = meta[0, g // 4, g % 4, b].astype(F32)
            local = m[:, 64:68] - (z * EXP).astype(F32)
            ids = local * 16.0 + b.astype(F32) * 4.0 + m[:, 80:84]
            ids = jnp.where((local >= 0.0) & (local < EXP), ids, -1.0)
            hit = slots == ids[:, 0:1]
            for k in range(1, 4):
                hit = hit | (slots == ids[:, k : k + 1])
            place[g, pl.ds(b * ROWS, ROWS), :] = hit.astype(F32).astype(BF16)
            return 0

        lax.fori_loop(0, 64, block, 0, unroll=4)

        def clear(e, _):
            acc[e] = jnp.zeros((256, 256), F32)
            return 0

        lax.fori_loop(0, EXP, clear, 0, unroll=4)

    @pl.when(step == 0)
    def _():
        def group(g, _):
            x = every[0, g // 4, g % 4].reshape(4 * ROWS, PW)
            picked = lax.dot_general(
                place[g], x, (((0,), (0,)), ((), ())), preferred_element_type=F32
            )
            rows[:, pl.ds(g * 16, 16), :] = picked.astype(BF16).reshape(EXP, 16, PW)
            return 0

        lax.fori_loop(0, 16, group, 0, unroll=4)

    for i in range(PER_STEP):
        e = step * PER_STEP + i
        acc[e, :, pl.ds(0, 4 * FP)] += lax.dot_general(
            rows[e],
            weights[i].reshape(4 * FP, PW),
            (((1,), (1,)), ((), ())),
            preferred_element_type=F32,
        )

    @pl.when(p == PARTS - 1)
    def _():
        ones = jnp.ones((128, 128), BF16)
        lane = lax.broadcasted_iota(jnp.int32, (256, 128), 1)
        for i in range(PER_STEP):
            e = step * PER_STEP + i
            total = acc[e]
            gate, up = total[:, :128], pltpu.roll(total, 128 - 2 * FP, 1)[:, 128:]
            m = rows[e, :, META:].astype(F32)
            named = pltpu.roll(m, 64, 1) == (z * EXP + e).astype(F32)
            chosen = jnp.where(named & (lane < 12), m, 0.0).astype(BF16)
            weight = jnp.dot(chosen, ones, preferred_element_type=F32)
            value = gate / (1.0 + jnp.exp(-gate)) * up * weight
            hidden[e] = value.astype(BF16)


def upward(every, weights):
    return pl.pallas_call(
        upward_kernel,
        grid=(PARTS, EXP // PER_STEP),
        out_shape=[
            jax.ShapeDtypeStruct((EXP, 256, 128), BF16),
            jax.ShapeDtypeStruct((16, 4 * ROWS, EXP * 16), BF16),
        ],
        in_specs=[
            pl.BlockSpec((1, 4, 4, 4, ROWS, PW), lambda p, s: (p, 0, 0, 0, 0, 0)),
            pl.BlockSpec((1, 4, 4, 4, ROWS, 128), lambda p, s: (2, 0, 0, 0, 0, 7)),
            pl.BlockSpec((PER_STEP, 2, 2 * FP, PW), lambda p, s: (s, 0, 0, p)),
        ],
        out_specs=[
            pl.BlockSpec((EXP, 256, 128), lambda p, s: (0, 0, 0)),
            pl.BlockSpec((16, 4 * ROWS, EXP * 16), lambda p, s: (0, 0, 0)),
        ],
        scratch_shapes=[
            pltpu.VMEM((EXP, 256, PW), BF16),
            pltpu.VMEM((EXP, 256, 256), F32),
        ],
        compiler_params=pltpu.CompilerParams(vmem_limit_bytes=VMEM),
    )(every, every, weights)


CHUNKS = 2
CW = PW // CHUNKS
BATCH = 8
BATCHES = EXP // BATCH
STAGES = 8


def downward_kernel(
    hidden, place, weights, out, part,
    far0, near0, mid0, acc, far1, near1, far2, near2, own2,
    results, stage, wbuf, sems, lsem, wsem, psem,
):
    me, core = position()
    parts = range(PARTS)
    sent = []

    def fetch(n):
        unit = n // BATCHES
        start = pl.multiple_of(unit % PARTS * PW + unit // PARTS * CW, CW)
        first = n % BATCHES * BATCH
        return pltpu.make_async_copy(
            weights.at[pl.ds(first, BATCH), 2, :, pl.ds(start, CW)], wbuf.at[n % 2], wsem.at[n % 2]
        )

    fetch(0).start()
    greet(me, core, False)

    def experts(c, p):
        def batch(s, _):
            n = (c * PARTS + p) * BATCHES + s
            fetch(n).wait()

            @pl.when(n + 1 < CHUNKS * PARTS * BATCHES)
            def _():
                fetch(n + 1).start()

            for i in range(BATCH):
                e = s * BATCH + i
                y = jnp.dot(
                    hidden[e, :, : 2 * FP], wbuf[n % 2, i], preferred_element_type=F32
                )
                first = pl.multiple_of(e * 16, 16)
                results[:, pl.ds(first, 16), :] = y.astype(BF16).reshape(16, 16, CW)
            return 0

        lax.fori_loop(0, BATCHES, batch, 0, unroll=2)

    def combine(c, p):
        def store(g):
            return pltpu.make_async_copy(
                stage.at[g % STAGES], part.at[c, p, g // 4, g % 4], psem.at[g % STAGES]
            )

        def group(g, _):
            @pl.when(g >= STAGES)
            def _():
                store(g - STAGES).wait()

            summed = jnp.dot(place[g], results[g], preferred_element_type=F32)
            stage[g % STAGES] = summed.astype(BF16).reshape(4, ROWS, CW)
            store(g).start()
            return 0

        lax.fori_loop(0, 16, group, 0, unroll=4)

        def stored(g, _):
            store(g).wait()
            return 0

        lax.fori_loop(16 - STAGES, 16, stored, 0)

    def copy(here, there, c, p, phase, kind, way, axis):
        return pltpu.make_async_remote_copy(
            here,
            there,
            sems.at[0, c, p, phase, kind],
            sems.at[1, c, p, phase, kind],
            device_id=device(moved(me, axis, way), core),
            device_id_type=MESH,
        )

    def go(*a):
        c = copy(*a)
        c.start()
        sent.append(c)

    def wait_in(there, c, p, phase, kind, axis):
        copy(there, there, c, p, phase, kind, 1, axis).wait_recv()

    top, bottom, whole = pl.ds(0, 32), pl.ds(32, 32), slice(None)

    def piece(c, p, jj, by, rows):
        o1, o2 = (p + 1) % 3, (p + 2) % 3
        index = [slice(None)] * 3
        index[o1] = (me[o1] + (2, 1, -1, 0)[jj] + 4) % 4
        index[o2] = (me[o2] + by + 4) % 4
        return part.at[(c, p, *index, rows)]

    def load(c, p, jj, k):
        by, rows = ((1, top), (-1, bottom), (0, whole))[k]
        there = acc.at[c, p, jj] if k == 2 else mid0.at[c, p, jj, k]
        return pltpu.make_async_copy(piece(c, p, jj, by, rows), there, lsem.at[c, p, jj, k])

    def issue(c, jj, which=parts):
        for p in which:
            axis = (p + 2) % 3
            go(piece(c, p, jj, 2, top), far0.at[c, p, jj, 0], c, p, jj, 0, 1, axis)
            go(piece(c, p, jj, 2, bottom), far0.at[c, p, jj, 1], c, p, jj, 1, -1, axis)
            for k in range(3):
                load(c, p, jj, k).start()
        for p in which:
            axis = (p + 2) % 3
            go(piece(c, p, jj, 1, bottom), near0.at[c, p, jj, 0, :, bottom], c, p, jj, 2, 1, axis)
            go(piece(c, p, jj, -1, top), near0.at[c, p, jj, 1, :, top], c, p, jj, 3, -1, axis)

    def add(target, *others):
        def one(i, _):
            total = target[i].astype(F32)
            for other in others:
                total = total + other[i].astype(F32)
            target[i] = total.astype(BF16)
            return 0

        lax.fori_loop(0, target.shape[0], one, 0)

    def middle(c, jj):
        for p in parts:
            axis = (p + 2) % 3
            for k, way in ((0, 1), (1, -1)):
                half = top if k == 0 else bottom
                load(c, p, jj, k).wait()
                wait_in(far0.at[c, p, jj, k], c, p, jj, k, axis)
                add(mid0.at[c, p, jj, k], far0.at[c, p, jj, k])
                go(mid0.at[c, p, jj, k], near0.at[c, p, jj, k, :, half], c, p, jj, 4 + k, way, axis)

    def collect(near, c, p, phase, axis, lead):
        for kind, k, half in ((2, 0, bottom), (3, 1, top), (4, 0, top), (5, 1, bottom)):
            wait_in(near.at[(*lead, k, *([whole] if phase < 5 else []), half)], c, p, phase, kind, axis)

    def finish(c, jj):
        for p in parts:
            load(c, p, jj, 2).wait()
            collect(near0, c, p, jj, (p + 2) % 3, (c, p, jj))
            add(acc.at[c, p, jj], near0.at[c, p, jj, 0], near0.at[c, p, jj, 1])
            axis = (p + 1) % 3
            if jj == 0:
                go(acc.at[c, p, 0, :, top], far1.at[c, p, 0], c, p, 4, 0, 1, axis)
                go(acc.at[c, p, 0, :, bottom], far1.at[c, p, 1], c, p, 4, 1, -1, axis)
            elif jj == 1:
                go(acc.at[c, p, 1, :, bottom], near1.at[c, p, 0, :, bottom], c, p, 4, 2, 1, axis)
            elif jj == 2:
                go(acc.at[c, p, 2, :, top], near1.at[c, p, 1, :, top], c, p, 4, 3, -1, axis)
        if jj in (1, 2):
            k, way, half = (0, 1, top) if jj == 1 else (1, -1, bottom)
            for p in parts:
                axis = (p + 1) % 3
                wait_in(far1.at[c, p, k], c, p, 4, k, axis)
                add(acc.at[c, p, jj, :, half], far1.at[c, p, k])
                go(acc.at[c, p, jj, :, half], near1.at[c, p, k, :, half], c, p, 4, 4 + k, way, axis)

    def lines(p):
        return [(me[p] + by + 4) % 4 for by in (2, 1, -1, 0)]

    def last_start(c):
        for p in parts:
            collect(near1, c, p, 4, (p + 1) % 3, (c, p))
            add(acc.at[c, p, 3], near1.at[c, p, 0], near1.at[c, p, 1])
            t = lines(p)
            go(acc.at[c, p, 3, t[0], top], far2.at[c, p, 0], c, p, 5, 0, 1, p)
            go(acc.at[c, p, 3, t[0], bottom], far2.at[c, p, 1], c, p, 5, 1, -1, p)
            go(acc.at[c, p, 3, t[1], bottom], near2.at[c, p, 0, bottom], c, p, 5, 2, 1, p)
            go(acc.at[c, p, 3, t[2], top], near2.at[c, p, 1, top], c, p, 5, 3, -1, p)

    def last_middle(c):
        for p in parts:
            t = lines(p)
            for k, way, half in ((0, 1, top), (1, -1, bottom)):
                wait_in(far2.at[c, p, k], c, p, 5, k, p)
                own2[c, p, k] = (
                    acc[c, p, 3, t[1 + k], half].astype(F32) + far2[c, p, k].astype(F32)
                ).astype(BF16)
                go(own2.at[c, p, k], near2.at[c, p, k, half], c, p, 5, 4 + k, way, p)

    def last_finish(c):
        for p in parts:
            collect(near2, c, p, 5, p, (c, p))
            out[c, p] = (
                acc[c, p, 3, me[p]].astype(F32)
                + near2[c, p, 0].astype(F32)
                + near2[c, p, 1].astype(F32)
            ).astype(BF16)

    for p in parts:
        experts(0, p)
        combine(0, p)
        issue(0, 0, (p,))
        issue(0, 1, (p,))
    experts(1, 0)
    middle(0, 0)
    issue(0, 2)
    combine(1, 0)
    issue(1, 0, (0,))
    middle(0, 1)
    issue(0, 3)
    experts(1, 1)
    finish(0, 0)
    combine(1, 1)
    issue(1, 0, (1,))
    middle(0, 2)
    experts(1, 2)
    finish(0, 1)
    middle(0, 3)
    combine(1, 2)
    issue(1, 0, (2,))
    issue(1, 1)
    finish(0, 2)
    finish(0, 3)
    middle(1, 0)
    issue(1, 2)
    last_start(0)
    middle(1, 1)
    issue(1, 3)
    last_middle(0)
    finish(1, 0)
    middle(1, 2)
    finish(1, 1)
    last_finish(0)
    middle(1, 3)
    finish(1, 2)
    finish(1, 3)
    last_start(1)
    last_middle(1)
    last_finish(1)
    for c in sent:
        c.wait_send()


def downward(hidden, place, weights):
    half = ROWS // 2
    vmem = pl.BlockSpec(memory_space=pltpu.VMEM)
    return pl.pallas_call(
        downward_kernel,
        out_shape=[
            jax.ShapeDtypeStruct((CHUNKS, PARTS, ROWS, CW), BF16),
            jax.ShapeDtypeStruct((CHUNKS, PARTS, 4, 4, 4, ROWS, CW), BF16),
        ],
        in_specs=[vmem, vmem, ANY],
        out_specs=[vmem, ANY],
        scratch_shapes=[
            pltpu.VMEM((CHUNKS, PARTS, 4, 2, 4, half, CW), BF16),
            pltpu.VMEM((CHUNKS, PARTS, 4, 2, 4, ROWS, CW), BF16),
            pltpu.VMEM((CHUNKS, PARTS, 4, 2, 4, half, CW), BF16),
            pltpu.VMEM((CHUNKS, PARTS, 4, 4, ROWS, CW), BF16),
            pltpu.VMEM((CHUNKS, PARTS, 2, 4, half, CW), BF16),
            pltpu.VMEM((CHUNKS, PARTS, 2, 4, ROWS, CW), BF16),
            pltpu.VMEM((CHUNKS, PARTS, 2, half, CW), BF16),
            pltpu.VMEM((CHUNKS, PARTS, 2, ROWS, CW), BF16),
            pltpu.VMEM((CHUNKS, PARTS, 2, half, CW), BF16),
            pltpu.VMEM((16, EXP * 16, CW), BF16),
            pltpu.VMEM((STAGES, 4, ROWS, CW), BF16),
            pltpu.VMEM((2, BATCH, 2 * FP, CW), BF16),
            pltpu.SemaphoreType.DMA((2, CHUNKS, PARTS, 6, 6)),
            pltpu.SemaphoreType.DMA((CHUNKS, PARTS, 4, 3)),
            pltpu.SemaphoreType.DMA((2,)),
            pltpu.SemaphoreType.DMA((STAGES,)),
        ],
        compiler_params=pltpu.CompilerParams(
            collective_id=2, has_side_effects=True, vmem_limit_bytes=VMEM
        ),
    )(hidden, place, weights)


def with_meta(tokens, routes, combine):
    flat = routes.reshape(-1)
    index = jnp.arange(flat.shape[0], dtype=jnp.int32)
    same = (flat[:, None] == flat[None, :]) & (index[None, :] < index[:, None])
    rank = jnp.sum(same.astype(jnp.int32), axis=1).reshape(routes.shape)
    high = lax.reduce_precision(combine, 8, 7)
    rest = combine - high
    middle = lax.reduce_precision(rest, 8, 7)
    low = rest - middle
    named = routes.astype(F32)
    columns = [high, middle, low, jnp.zeros((ROWS, 52), F32), named, named, named]
    columns += [jnp.zeros((ROWS, 4), F32), rank.astype(F32), jnp.zeros((ROWS, 44), F32)]
    meta = jnp.concatenate(columns, axis=1).astype(BF16)
    pad = jnp.zeros((ROWS, PARTS * PW - 128 - D), BF16)
    wide = jnp.concatenate([tokens, pad, meta], axis=1)
    return wide.reshape(ROWS, PARTS, PW).transpose(1, 0, 2)


def local(tokens, routes, combine, gv, gs, uv, us, dv, ds):
    weights = [w.transpose(1, 0, 2) for w in (gv, gs, uv, us, dv, ds)]
    every, ready = gather(with_meta(tokens, routes, combine), *weights)
    hidden, place = upward(every, ready)
    result = downward(hidden, place, ready)[0]
    return result.transpose(2, 1, 0, 3).reshape(ROWS, PARTS * PW)[:, :D]


def solution(mesh):
    rows = P(("eg", "tp"), None)
    weight = P("tp", "eg", None)
    return jax.shard_map(
        local,
        mesh=mesh,
        in_specs=(rows, rows, rows) + (weight,) * 6,
        out_specs=rows,
        check_vma=False,
    )
```
